32 devices in a mesh: gx: 16 (over z, y, core), gy: 2 (over x).
Axes of the slice: x: 2, y: 2, z: 4, core: 2. Of those that a mesh axis runs over, the one named last changes fastest.
Arguments:
- features: bfloat16 [8192, 8, 8, 256], P('gx', 'gy'), may hold values from -6 to 6
- spectral_weight: bfloat16 [16, 2, 256, 256], replicated, may hold values from -6 to 6
- conv_taps: float32 [3, 256], replicated, may hold values from -3 to 3
- w_in: bfloat16 [256, 1024], replicated, may hold values from -0.375 to 0.375
- bias_in: float32 [1024], replicated, may hold values from -3 to 3
- w_out: bfloat16 [1024, 256], replicated, may hold values from -0.1875 to 0.1875
- bias_out: float32 [256], replicated, may hold values from -3 to 3
Outputs:
- layer_out: bfloat16 [8192, 8, 8, 256], P('gx', 'gy')
The draws below stay inside these ranges and needn't reach their ends.
All inputs are finite; a program needn't handle non-finite values.
Results may differ from the reference program's by a relative error of at most 0.0065.
Values may be sent and summed in bfloat16 or wider, within the bound.
No kernel may reach another device: no remote copies, remote signals or barrier semaphores. Data moves between devices by JAX's collectives and lax.ppermute only.
A program may use at most 128 MiB of HBM per device.

```python
import math
import jax
import jax.numpy as jnp
from jax import lax

C = 256
HID = 1024
MODES = 16
X = 8192
Z = 8
Y = 8


def block_levels(key, dims, cuts, low, largest):
    gain = 1.0
    for axis_at, shards_of in cuts:
        steps = jax.random.uniform(jax.random.fold_in(jax.random.fold_in(key, 6), axis_at), (shards_of,), jnp.float32, low / len(cuts), largest / len(cuts))
        gain = gain * jnp.repeat(jnp.exp(steps), dims[axis_at] // shards_of).reshape((-1,) + (1,) * (len(dims) - 1 - axis_at))
    return gain


def scatter_about(own_key, dims, spread, limit, cuts=(), held_as=jnp.bfloat16):
    loudness = block_levels(own_key, dims, cuts, -0.22, 0.18) if cuts else 1.0
    array = jax.random.normal(own_key, dims, jnp.float32) * spread * loudness
    return jnp.minimum(jnp.maximum(array, -limit), limit).astype(held_as)


def setup_inputs(seed: int = 0) -> dict:
    streams_of = jax.random.split(jax.random.key(seed), 8)
    return {
        "features": scatter_about(streams_of[0], (X, Y, Z, C), 1.0, 6.0, ((0, 16), (1, 2))),
        "spectral_weight": scatter_about(streams_of[1], (MODES, 2, C, C), 1.0, 6.0),
        "conv_taps": scatter_about(streams_of[2], (3, C), 0.5, 3.0, (), jnp.float32),
        "w_in": scatter_about(streams_of[3], (C, HID), C ** -0.5, 0.375),
        "bias_in": scatter_about(streams_of[4], (HID,), 0.5, 3.0, (), jnp.float32),
        "w_out": scatter_about(streams_of[5], (HID, C), HID ** -0.5, 0.1875),
        "bias_out": scatter_about(streams_of[6], (C,), 0.5, 3.0, (), jnp.float32),
    }


def make_tables(positions, total, mode_count):
    waves = jnp.arange(mode_count, dtype=jnp.int32)
    product = waves[:, None] * positions[None, :] % total
    angles = 2.0 * math.pi / total * product.astype(jnp.float32)
    scale = 1.0 / math.sqrt(total)
    cosines = jnp.cos(angles)
    sines = jnp.sin(angles)
    forward = (jnp.concatenate([cosines, -sines], 0) * scale).astype(jnp.bfloat16)
    amplitude = jnp.where(waves == 0, 1.0, 2.0).astype(jnp.float32)[:, None]
    inverse = (jnp.concatenate([amplitude * cosines, -amplitude * sines], 0) * scale).T.astype(jnp.bfloat16)
    return (forward, inverse)

def reference(features, spectral_weight, conv_taps, w_in, bias_in, w_out, bias_out):
    positions = jnp.arange(X, dtype=jnp.int32)
    forward, inverse = make_tables(positions, X, MODES)
    weight_real = spectral_weight[:, 0].astype(jnp.float32)
    weight_imag = spectral_weight[:, 1].astype(jnp.float32)

    def column(index):
        plane = lax.dynamic_index_in_dim(features, index, 2, keepdims=False)
        flattened = plane.reshape(X, Y * C)
        spectrum = jnp.dot(forward, flattened, preferred_element_type=jnp.float32)
        spectrum_b = spectrum.astype(jnp.bfloat16).astype(jnp.float32).reshape(2, MODES, Y, C)
        mixed_real = jnp.einsum('kyc,kco->kyo', spectrum_b[0], weight_real) - jnp.einsum('kyc,kco->kyo', spectrum_b[1], weight_imag)
        mixed_imag = jnp.einsum('kyc,kco->kyo', spectrum_b[0], weight_imag) + jnp.einsum('kyc,kco->kyo', spectrum_b[1], weight_real)
        mixed = jnp.stack([mixed_real, mixed_imag]).astype(jnp.bfloat16).reshape(2 * MODES, Y * C)
        spectral = jnp.dot(inverse, mixed, preferred_element_type=jnp.float32).reshape(X, Y, C)
        padded = jnp.pad(plane.astype(jnp.float32), ((0, 0), (1, 1), (0, 0)))
        conv = conv_taps[0] * padded[:, :-2] + conv_taps[1] * padded[:, 1:-1] + conv_taps[2] * padded[:, 2:]
        joined = (spectral + conv).astype(jnp.bfloat16).reshape(X * Y, C)
        hidden = jax.nn.gelu(jnp.dot(joined, w_in, preferred_element_type=jnp.float32) + bias_in, approximate=True).astype(jnp.bfloat16)
        result = plane.astype(jnp.float32).reshape(X * Y, C) + jnp.dot(hidden, w_out, preferred_element_type=jnp.float32) + bias_out
        return result.astype(jnp.bfloat16).reshape(X, Y, C)
    stacked = lax.map(column, jnp.arange(Z, dtype=jnp.int32))
    return jnp.transpose(stacked, (1, 2, 0, 3))
```

```python
import functools
import math

import jax
import jax.numpy as jnp
from jax import lax
from jax.experimental import pallas as pl
from jax.experimental.pallas import tpu as pltpu
from jax.sharding import PartitionSpec as P

F32 = jnp.float32
BF16 = jnp.bfloat16
GELU_A = math.sqrt(2.0 / math.pi)
GELU_B = GELU_A * 0.044715
VMEM_BYTES = 50 * 2**20


def wave_tables(waves, positions, total):
    product = waves[:, None] * positions[None, :] % total
    angles = 2.0 * math.pi / total * product.astype(F32)
    scale = 1.0 / math.sqrt(total)
    cosines = jnp.cos(angles)
    sines = jnp.sin(angles)
    forward = (jnp.stack([cosines, -sines], 1) * scale).astype(BF16)
    amplitude = jnp.where(waves == 0, 1.0, 2.0).astype(F32)[:, None]
    inverse = (jnp.stack([amplitude * cosines, -amplitude * sines], 1) * scale).astype(BF16)
    rows = 2 * waves.shape[0]
    return forward.reshape(rows, -1), inverse.reshape(rows, -1)


def forward_kernel(half, table_ref, inverse_ref, field_ref, send_ref, keep_ref, inv_ref, total_ref):
    step = pl.program_id(0)
    xb, rows, cols, channels = field_ref.shape
    waves = table_ref.shape[1]
    width = xb * cols
    spread = (
        lax.broadcasted_iota(jnp.int32, (xb, width), 1) // cols
        == lax.broadcasted_iota(jnp.int32, (xb, width), 0)
    )
    wide = jnp.dot(table_ref[0], spread.astype(F32).astype(BF16), preferred_element_type=F32)
    same = lax.broadcasted_iota(jnp.int32, (1, cols, width), 2) % cols == lax.broadcasted_iota(
        jnp.int32, (1, cols, width), 1
    )
    wide = jnp.where(same, wide[:, None, :], 0.0).reshape(waves * cols, width).astype(BF16)

    @pl.when(step == 0)
    def _():
        total_ref[...] = jnp.zeros_like(total_ref)

    for row in range(rows):
        block = field_ref[:, row].reshape(width, channels)
        total_ref[row] += jnp.dot(wide, block, preferred_element_type=F32)

    columns = waves * cols
    spread = (
        lax.broadcasted_iota(jnp.int32, (waves, columns), 1) // cols
        == lax.broadcasted_iota(jnp.int32, (waves, columns), 0)
    )
    tall = jnp.dot(inverse_ref[...], spread.astype(F32).astype(BF16), preferred_element_type=F32)
    same = lax.broadcasted_iota(jnp.int32, (1, cols, columns), 2) % cols == lax.broadcasted_iota(
        jnp.int32, (1, cols, columns), 1
    )
    tall = jnp.where(same, tall[:, None, :], 0.0).reshape(width, columns)
    inv_ref[...] = tall.astype(BF16)

    @pl.when(step == pl.num_programs(0) - 1)
    def _():
        for row in range(rows):
            part = total_ref[row].reshape(waves, cols, channels)
            keep_ref[:, row] = part[:half]
            send_ref[:, row] = part[half:].astype(BF16)


def forward_transform(features, table, inverse, xb, half):
    x_rows, y_rows, cols, channels = features.shape
    waves = inverse.shape[1]
    steps = x_rows // xb
    shape = (half, y_rows, cols, channels)
    rest = (waves - half, y_rows, cols, channels)
    whole = lambda i: (0, 0, 0, 0)
    return pl.pallas_call(
        functools.partial(forward_kernel, half),
        grid=(steps,),
        in_specs=[
            pl.BlockSpec((1, waves, xb), lambda i: (i, 0, 0)),
            pl.BlockSpec((xb, waves), lambda i: (i, 0)),
            pl.BlockSpec((xb, y_rows, cols, channels), lambda i: (i, 0, 0, 0)),
        ],
        out_specs=[
            pl.BlockSpec(rest, whole),
            pl.BlockSpec(shape, whole),
            pl.BlockSpec((xb * cols, waves * cols), lambda i: (i, 0)),
        ],
        out_shape=[
            jax.ShapeDtypeStruct(rest, BF16),
            jax.ShapeDtypeStruct(shape, F32),
            jax.ShapeDtypeStruct((x_rows * cols, waves * cols), BF16),
        ],
        scratch_shapes=[pltpu.VMEM((y_rows, waves * cols, channels), F32)],
        compiler_params=pltpu.CompilerParams(vmem_limit_bytes=VMEM_BYTES),
        cost_estimate=pl.CostEstimate(
            flops=2 * x_rows * y_rows * cols * cols * waves * channels,
            bytes_accessed=features.size * 2,
            transcendentals=0,
        ),
        name="forward",
    )(table, inverse, features)


def halve_kernel(half, keep_ref, got_ref, send_ref, next_ref):
    next_ref[...] = keep_ref[:half] + got_ref[:half].astype(F32)
    send_ref[...] = (keep_ref[half:] + got_ref[half:].astype(F32)).astype(BF16)


def halve(keep, got):
    half = keep.shape[0] // 2
    shape = (half,) + keep.shape[1:]
    return pl.pallas_call(
        functools.partial(halve_kernel, half),
        out_shape=[jax.ShapeDtypeStruct(shape, BF16), jax.ShapeDtypeStruct(shape, F32)],
        compiler_params=pltpu.CompilerParams(vmem_limit_bytes=VMEM_BYTES),
        name="halve",
    )(keep, got)


def add_kernel(keep_ref, got_ref, send_ref, next_ref):
    total = keep_ref[...] + got_ref[...].astype(F32)
    next_ref[...] = total
    send_ref[...] = total.astype(BF16)


def add(keep, got):
    return pl.pallas_call(
        add_kernel,
        out_shape=[
            jax.ShapeDtypeStruct(keep.shape, BF16),
            jax.ShapeDtypeStruct(keep.shape, F32),
        ],
        compiler_params=pltpu.CompilerParams(vmem_limit_bytes=VMEM_BYTES),
        name="add",
    )(keep, got)


def mix_kernel(which_ref, keep_ref, got_ref, weight_ref, out_ref):
    modes = weight_ref.shape[0]
    waves, rows, cols, channels = keep_ref.shape
    count = rows * cols
    for mode in range(modes):
        parts = []
        for p in range(2):
            at = 2 * mode + p
            part = keep_ref[at] + got_ref[at].astype(F32)
            parts.append(part.reshape(count, channels).astype(BF16))
        real, imag = parts
        weight_real = weight_ref[mode, 0]
        weight_imag = weight_ref[mode, 1]
        dot = functools.partial(jnp.dot, preferred_element_type=F32)
        mixed_real = dot(real, weight_real) - dot(imag, weight_imag)
        mixed_imag = dot(real, weight_imag) + dot(imag, weight_real)
        out_ref[2 * mode] = mixed_real.reshape(rows, cols, channels).astype(BF16)
        out_ref[2 * mode + 1] = mixed_imag.reshape(rows, cols, channels).astype(BF16)


def mix(keep, got, weight, which):
    waves, rows, cols, channels = keep.shape
    modes = waves // 2
    whole = lambda i, w: (0, 0, 0, 0)
    return pl.pallas_call(
        mix_kernel,
        grid_spec=pltpu.PrefetchScalarGridSpec(
            num_scalar_prefetch=1,
            grid=(1,),
            in_specs=[
                pl.BlockSpec(keep.shape, whole),
                pl.BlockSpec(keep.shape, whole),
                pl.BlockSpec((modes, 2, channels, channels), lambda i, w: (w[0], 0, 0, 0)),
            ],
            out_specs=pl.BlockSpec(keep.shape, whole),
        ),
        out_shape=jax.ShapeDtypeStruct(keep.shape, BF16),
        compiler_params=pltpu.CompilerParams(vmem_limit_bytes=VMEM_BYTES),
        name="mix",
    )(which, keep, got, weight)


def row_kernel(
    pieces, sub, rows_ref, before_ref, here_ref, after_ref, inv_ref, taps_ref,
    w_in_ref, bias_in_ref, w_out_ref, bias_out_ref, *rest
):
    piece_refs = rest[:pieces]
    out_ref, mixed_ref, joined_ref, hidden_ref = rest[-4:]
    xb = here_ref.shape[0]
    cols, channels = here_ref.shape[-2:]
    tokens = xb * cols

    @pl.when(pl.program_id(1) == 0)
    def _():
        at = 0
        for ref in piece_refs:
            count = ref.shape[0] * cols
            piece = ref[...].astype(F32).reshape(count, channels).astype(BF16)
            mixed_ref[at : at + count] = piece
            at += count

    taps = taps_ref[0]

    def load(ref, s):
        part = ref[s * sub // cols : (s + 1) * sub // cols]
        return part.reshape(sub, channels)

    def join(s):
        rows = slice(s * sub, (s + 1) * sub)
        spectral = jnp.dot(inv_ref[rows], mixed_ref[...], preferred_element_type=F32)
        conv = (
            taps[0:1] * load(before_ref, s).astype(F32)
            + taps[1:2] * load(here_ref, s).astype(F32)
            + taps[2:3] * load(after_ref, s).astype(F32)
        )
        joined_ref[rows] = (spectral + conv).astype(BF16)

    def expand(s):
        rows = slice(s * sub, (s + 1) * sub)
        x = jnp.dot(joined_ref[rows], w_in_ref[...], preferred_element_type=F32)
        x = (x + bias_in_ref[...]).astype(BF16)
        u = x * (BF16(GELU_A) + BF16(GELU_B) * (x * x))
        hidden_ref[rows] = x + x * jnp.tanh(u)

    def project(s):
        rows = slice(s * sub, (s + 1) * sub)
        y = jnp.dot(hidden_ref[rows], w_out_ref[...], preferred_element_type=F32)
        y = load(here_ref, s).astype(F32) + (0.5 * y + bias_out_ref[...])
        out_ref[s * sub // cols : (s + 1) * sub // cols] = y.reshape(
            (sub // cols,) + out_ref.shape[1:]
        ).astype(BF16)

    parts = tokens // sub
    for s in range(parts + 2):
        if s < parts:
            join(s)
        if 0 <= s - 1 < parts:
            expand(s - 1)
        if s >= 2:
            project(s - 2)


def rows_of(out, features, inv, taps, rows, w_in, bias_in, w_out, bias_out, pieces, xb, start, count, halo=None):
    x_rows, y_rows, cols, channels = features.shape
    hidden = w_in.shape[1]
    waves_cols = inv.shape[1]
    slots = taps.shape[0]
    block = (xb, 1, cols, channels)
    first = start // xb
    at = lambda which: pl.BlockSpec(block, lambda s, i, r: (i + first, r[which, s], 0, 0))
    fixed = lambda shape: pl.BlockSpec(shape, lambda s, i, r: (0,) * len(shape))
    if halo is None:
        after, after_spec = features, at(2)
    else:
        after, after_spec = halo, pl.BlockSpec((xb, cols, channels), lambda s, i, r: (i, 0, 0))
    piece_specs = [
        pl.BlockSpec((p.shape[0], 1, cols, channels), lambda s, i, r: (0, r[1, s], 0, 0))
        for p in pieces
    ]
    tokens = xb * cols
    sub = min(512, tokens)
    in_specs = [
        at(0),
        at(1),
        after_spec,
        pl.BlockSpec((tokens, waves_cols), lambda s, i, r: (i + first, 0)),
        pl.BlockSpec((1, 3, channels), lambda s, i, r: (s, 0, 0)),
        fixed((channels, hidden)),
        fixed((1, hidden)),
        fixed((hidden, channels)),
        fixed((1, channels)),
        *piece_specs,
    ]
    args = [rows, features, features, after, inv, taps, w_in, bias_in, w_out, bias_out, *pieces]
    aliases = {}
    if out is not None:
        aliases = {len(args): 0}
        in_specs.append(pl.BlockSpec(memory_space=pl.ANY))
        args.append(out)
    work = slots * count * cols
    return pl.pallas_call(
        functools.partial(row_kernel, len(pieces), sub),
        grid_spec=pltpu.PrefetchScalarGridSpec(
            num_scalar_prefetch=1,
            grid=(slots, count // xb),
            in_specs=in_specs,
            out_specs=at(1),
            scratch_shapes=[
                pltpu.VMEM((waves_cols, channels), BF16),
                pltpu.VMEM((tokens, channels), BF16),
                pltpu.VMEM((tokens, hidden), BF16),
            ],
        ),
        out_shape=jax.ShapeDtypeStruct(features.shape, BF16),
        input_output_aliases=aliases,
        compiler_params=pltpu.CompilerParams(vmem_limit_bytes=VMEM_BYTES),
        cost_estimate=pl.CostEstimate(
            flops=2 * work * channels * (2 * hidden + waves_cols),
            bytes_accessed=work * channels * 10,
            transcendentals=work * hidden,
        ),
        name="rows" if halo is None else "halo_rows",
    )(*args)


def chunks_of(x_rows):
    unit = x_rows // 8
    return [(0, 3 * unit), (3 * unit, 3 * unit), (6 * unit, 2 * unit)]


def local(features, spectral_weight, conv_taps, w_in, bias_in, w_out, bias_out):
    x_rows, y_rows, cols, channels = features.shape
    modes = spectral_weight.shape[0]
    gx_size = lax.axis_size("gx")
    gy_size = lax.axis_size("gy")
    gx = lax.axis_index("gx")
    gy = lax.axis_index("gy")

    edges = [jnp.where(gy % 2 == p, y_rows - 1, 0) for p in range(2)]
    live = [gy_size > p + 1 for p in range(2)]
    halos = [[], []]
    for p in range(2):
        if live[p]:
            swaps = [(a, b) for i in range(p, gy_size - 1, 2) for a, b in ((i, i + 1), (i + 1, i))]
            for start, count in chunks_of(x_rows):
                edge = lax.dynamic_slice(
                    features, (start, edges[p], 0, 0), (count, 1, cols, channels)
                ).reshape(count, cols, channels)
                halos[p].append(lax.ppermute(edge, "gy", swaps))

    levels = gx_size.bit_length() - 1
    halving = max(min(levels - 1, modes.bit_length() - 1), 0)
    own = jnp.int32(0)
    for level in range(halving):
        own = own + (gx >> level & 1) * (modes >> level + 1)
    waves = jnp.arange(modes, dtype=jnp.int32) ^ own
    positions = gx * x_rows + jnp.arange(x_rows, dtype=jnp.int32)
    table, inverse = wave_tables(waves, positions, x_rows * gx_size)
    xb = x_rows // 8
    table = table.reshape(2 * modes, 8, xb).transpose(1, 0, 2)
    swap = lambda a, level: lax.ppermute(
        a, "gx", [(i, i ^ (1 << level)) for i in range(gx_size)]
    )
    send, keep, inv = forward_transform(features, table, inverse.T, xb, modes)
    for level in range(halving):
        got = swap(send, level)
        if level + 1 < halving:
            send, keep = halve(keep, got)
        else:
            send, keep = add(keep, got)
    for level in range(halving, levels):
        got = swap(send, level)
        if level + 1 < levels:
            send, keep = add(keep, got)
    owned = modes >> halving
    which = (own // owned).reshape(1)
    pieces = [mix(keep, got, spectral_weight, which)]
    for level in reversed(range(halving)):
        pieces = pieces + [swap(p, level) for p in pieces]

    def neighbours(row, outer_live):
        first = row == 0
        last = row == y_rows - 1
        before = jnp.where(first, row if not outer_live else row + 1, row - 1)
        return before

    none = jnp.zeros_like(conv_taps[0])
    rows, taps = [], []
    for row in range(1, y_rows - 1):
        rows.append(jnp.stack([jnp.int32(v) for v in (row - 1, row, row + 1)]))
        taps.append(conv_taps)
    edge_args = []
    for p in range(2):
        top = edges[p] == 0
        inner = jnp.where(top, 1, y_rows - 2)
        inner_tap = jnp.where(top, conv_taps[2], conv_taps[0])
        outer_tap = jnp.where(top, conv_taps[0], conv_taps[2])
        index = jnp.stack([inner, edges[p], edges[p]]).astype(jnp.int32)
        if live[p]:
            edge_args.append((p, index, jnp.stack([inner_tap, conv_taps[1], outer_tap])))
        else:
            rows.append(index)
            taps.append(jnp.stack([inner_tap, conv_taps[1], none]))
    dense = (w_in, bias_in[None], w_out, bias_out[None], pieces)
    out = None
    if rows:
        out = rows_of(
            None, features, inv, jnp.stack(taps), jnp.stack(rows, 1), *dense, x_rows // 2, 0, x_rows
        )
    for at, (start, count) in enumerate(chunks_of(x_rows)):
        for p, index, tap in edge_args:
            out = rows_of(
                out, features, inv, tap[None], index[:, None], *dense, xb, start, count, halos[p][at]
            )
    return out


def solution(mesh):
    return jax.shard_map(
        local,
        mesh=mesh,
        in_specs=(P("gx", "gy", None, None), P(), P(), P(), P(), P(), P()),
        out_specs=P("gx", "gy", None, None),
        check_vma=False,
    )
```

```python
import functools
import math

import jax
import jax.numpy as jnp
from jax import lax
from jax.experimental import pallas as pl
from jax.experimental.pallas import tpu as pltpu
from jax.sharding import PartitionSpec as P

F32 = jnp.float32
BF16 = jnp.bfloat16
GELU_A = math.sqrt(2.0 / math.pi)
GELU_B = GELU_A * 0.044715
SMALL_BYTES = 16 * 2**20
ROWS_BYTES = 36 * 2**20


def wave_tables(own, start, modes, x_rows, total):
    shape = (2 * modes, x_rows)
    row = lax.broadcasted_iota(jnp.int32, shape, 0)
    waves = row // 2 ^ own
    product = waves * (start + lax.broadcasted_iota(jnp.int32, shape, 1)) % total
    angles = 2.0 * math.pi / total * product.astype(F32)
    scale = 1.0 / math.sqrt(total)
    parts = jnp.where(row % 2 == 0, jnp.cos(angles), -jnp.sin(angles))
    amplitude = jnp.where(waves == 0, 1.0, 2.0).astype(F32)
    return (parts * scale).astype(BF16), (amplitude * parts * scale).astype(BF16)


def spread(table, cols):
    waves, xb = table.shape
    columns = waves * cols
    place = (
        lax.broadcasted_iota(jnp.int32, (waves, columns), 1) // cols
        == lax.broadcasted_iota(jnp.int32, (waves, columns), 0)
    )
    tall = lax.dot_general(
        table, place.astype(F32).astype(BF16), (((0,), (0,)), ((), ())), preferred_element_type=F32
    )
    same = lax.broadcasted_iota(jnp.int32, (1, cols, columns), 2) % cols == lax.broadcasted_iota(
        jnp.int32, (1, cols, columns), 1
    )
    return jnp.where(same, tall[:, None, :], 0.0).reshape(xb * cols, columns).astype(BF16)


def spread_wide(table, cols):
    waves, xb = table.shape
    width = xb * cols
    place = (
        lax.broadcasted_iota(jnp.int32, (xb, width), 1) // cols
        == lax.broadcasted_iota(jnp.int32, (xb, width), 0)
    )
    wide = jnp.dot(table, place.astype(F32).astype(BF16), preferred_element_type=F32)
    same = lax.broadcasted_iota(jnp.int32, (1, cols, width), 2) % cols == lax.broadcasted_iota(
        jnp.int32, (1, cols, width), 1
    )
    return jnp.where(same, wide[:, None, :], 0.0).reshape(waves * cols, width).astype(BF16)


def cut_kernel(p, start, rows_ref, variant_ref, field_ref, ahead_ref, cut_ref):
    row = rows_ref[variant_ref[0], p]
    cut_ref[...] = field_ref[start : start + cut_ref.shape[0], row]


def cut_edge(field, rows, variant, p, part, parts, ahead):
    x_rows, _, cols, channels = field.shape
    count = x_rows // parts
    return pl.pallas_call(
        functools.partial(cut_kernel, p, part * count),
        in_specs=[
            pl.BlockSpec(memory_space=pltpu.SMEM),
            pl.BlockSpec(memory_space=pltpu.SMEM),
            pl.BlockSpec(memory_space=pltpu.VMEM),
            pl.BlockSpec(memory_space=pl.ANY),
        ],
        out_specs=pl.BlockSpec(memory_space=pltpu.VMEM),
        out_shape=jax.ShapeDtypeStruct((count, cols, channels), BF16),
        compiler_params=pltpu.CompilerParams(vmem_limit_bytes=SMALL_BYTES),
        name="cut",
    )(rows, variant, field, ahead)


def widen_kernel(table_ref, wide_ref):
    x_rows = table_ref.shape[1]
    cols = wide_ref.shape[1] // x_rows
    xb = min(x_rows, 128)
    width = xb * cols
    for part in range(x_rows // xb):
        wide_ref[:, part * width : (part + 1) * width] = spread_wide(
            table_ref[:, part * xb : (part + 1) * xb], cols
        )


def widen(table, cols):
    waves, x_rows = table.shape
    return pl.pallas_call(
        widen_kernel,
        out_shape=jax.ShapeDtypeStruct((waves * cols, x_rows * cols), BF16),
        compiler_params=pltpu.CompilerParams(vmem_limit_bytes=SMALL_BYTES),
        cost_estimate=pl.CostEstimate(
            flops=10**9, bytes_accessed=4 * waves * cols * x_rows * cols, transcendentals=0
        ),
        name="widen",
    )(table)


def forward_kernel(rows_ref, variant_ref, wide_ref, field_ref, send_ref, keep_ref):
    x_rows, y_rows, cols, channels = field_ref.shape
    sent = send_ref.shape[1]
    waves = send_ref.shape[0]
    for place in range(y_rows):
        row = rows_ref[variant_ref[0], place]
        part = jnp.dot(
            wide_ref[...],
            field_ref[:, row].reshape(x_rows * cols, channels),
            preferred_element_type=F32,
        ).reshape(waves, cols, channels)
        if place < sent:
            send_ref[:, place] = part.astype(BF16)
        else:
            keep_ref[:, place - sent] = part


def forward_transform(features, wide, rows, variant):
    x_rows, y_rows, cols, channels = features.shape
    shape = (wide.shape[0] // cols, y_rows // 2, cols, channels)
    vmem = pl.BlockSpec(memory_space=pltpu.VMEM)
    smem = pl.BlockSpec(memory_space=pltpu.SMEM)
    return pl.pallas_call(
        forward_kernel,
        in_specs=[smem, smem, vmem, vmem],
        out_specs=[vmem, vmem],
        out_shape=[jax.ShapeDtypeStruct(shape, BF16), jax.ShapeDtypeStruct(shape, F32)],
        compiler_params=pltpu.CompilerParams(vmem_limit_bytes=SMALL_BYTES),
        name="forward",
    )(rows, variant, wide, features)


def prepare_kernel(which_ref, table_ref, weight_ref, inv_ref, own_ref, sem):
    owned = own_ref.shape[0]
    move = pltpu.make_async_copy(weight_ref.at[pl.ds(which_ref[0], owned)], own_ref, sem)
    move.start()
    waves, x_rows = table_ref.shape
    cols = inv_ref.shape[0] // x_rows
    xb = min(x_rows, 128)
    for part in range(x_rows // xb):
        inv_ref[part * xb * cols : (part + 1) * xb * cols] = spread(
            table_ref[:, part * xb : (part + 1) * xb], cols
        )
    move.wait()


def prepare(table, cols, weight, which, owned):
    waves, x_rows = table.shape
    vmem = pl.BlockSpec(memory_space=pltpu.VMEM)
    return pl.pallas_call(
        prepare_kernel,
        in_specs=[
            pl.BlockSpec(memory_space=pltpu.SMEM),
            vmem,
            pl.BlockSpec(memory_space=pltpu.HBM),
        ],
        out_specs=[vmem, vmem],
        out_shape=[
            jax.ShapeDtypeStruct((x_rows * cols, waves * cols), BF16),
            jax.ShapeDtypeStruct((owned,) + weight.shape[1:], BF16),
        ],
        scratch_shapes=[pltpu.SemaphoreType.DMA],
        compiler_params=pltpu.CompilerParams(vmem_limit_bytes=SMALL_BYTES),
        name="prepare",
    )(which, table, weight)


def halve_kernel(half, keep_ref, got_ref, *refs):
    send_ref, next_ref = refs[-2:]
    next_ref[...] = keep_ref[:half] + got_ref[:half].astype(F32)
    send_ref[...] = (keep_ref[half:] + got_ref[half:].astype(F32)).astype(BF16)


def add_kernel(keep_ref, got_ref, *refs):
    send_ref, next_ref = refs[-2:]
    total = keep_ref[...] + got_ref[...].astype(F32)
    next_ref[...] = total
    send_ref[...] = total.astype(BF16)


def combine(keep, got, halve, ahead):
    half = keep.shape[0] // 2 if halve else keep.shape[0]
    shape = (half,) + keep.shape[1:]
    vmem = pl.BlockSpec(memory_space=pltpu.VMEM)
    return pl.pallas_call(
        functools.partial(halve_kernel, half) if halve else add_kernel,
        in_specs=[vmem, vmem] + [pl.BlockSpec(memory_space=pl.ANY)] * len(ahead),
        out_specs=[vmem, vmem],
        out_shape=[jax.ShapeDtypeStruct(shape, BF16), jax.ShapeDtypeStruct(shape, F32)],
        compiler_params=pltpu.CompilerParams(vmem_limit_bytes=SMALL_BYTES),
        name="halve" if halve else "add",
    )(keep, got, *ahead)


def join_kernel(mine_ref, got_ref, out_ref):
    half = mine_ref.shape[0]
    out_ref[:half] = mine_ref[...]
    out_ref[half:] = got_ref[...]


def join(mine, got):
    return pl.pallas_call(
        join_kernel,
        out_shape=jax.ShapeDtypeStruct((2 * mine.shape[0],) + mine.shape[1:], BF16),
        compiler_params=pltpu.CompilerParams(vmem_limit_bytes=SMALL_BYTES),
        name="join",
    )(mine, got)


def stack_kernel(*refs):
    out_ref = refs[-1]
    rows, _, channels = out_ref.shape
    at = 0
    for ref in refs[:-1]:
        count = ref.shape[0] * ref.shape[2]
        for row in range(rows):
            out_ref[row, at : at + count] = ref[:, row].reshape(count, channels)
        at += count


def stack_modes(pieces):
    waves = sum(p.shape[0] for p in pieces)
    _, rows, cols, channels = pieces[0].shape
    return pl.pallas_call(
        stack_kernel,
        out_shape=jax.ShapeDtypeStruct((rows, waves * cols, channels), BF16),
        compiler_params=pltpu.CompilerParams(vmem_limit_bytes=SMALL_BYTES),
        name="stack",
    )(*pieces)


def mix_kernel(keep_ref, got_ref, weight_ref, out_ref):
    modes = weight_ref.shape[0]
    _, rows, cols, channels = keep_ref.shape
    count = rows * cols
    dot = functools.partial(jnp.dot, preferred_element_type=F32)
    for mode in range(modes):
        both = slice(2 * mode, 2 * mode + 2)
        parts = keep_ref[both] + got_ref[both].astype(F32)
        parts = parts.reshape(2 * count, channels).astype(BF16)
        by_real = dot(parts, weight_ref[mode, 0])
        by_imag = dot(parts, weight_ref[mode, 1])
        mixed_real = by_real[:count] - by_imag[count:]
        mixed_imag = by_imag[:count] + by_real[count:]
        out_ref[2 * mode] = mixed_real.reshape(rows, cols, channels).astype(BF16)
        out_ref[2 * mode + 1] = mixed_imag.reshape(rows, cols, channels).astype(BF16)


def mix(keep, got, weight):
    return pl.pallas_call(
        mix_kernel,
        out_shape=jax.ShapeDtypeStruct(keep.shape, BF16),
        compiler_params=pltpu.CompilerParams(vmem_limit_bytes=SMALL_BYTES),
        name="mix",
    )(keep, got, weight)


BEFORE, HERE, AFTER, BLOCK, PLACE, GROUP, HALO, FLIP, DROP = range(9)


def row_kernel(
    halos, sub, items_ref, variant_ref, field_ref, inv_ref, taps_ref,
    w_in_ref, bias_in_ref, w_out_ref, bias_out_ref, mine_ref, other_ref, *rest
):
    halo_refs = rest[:halos]
    out_ref, mixed_ref, joined_ref, hidden_ref = rest[-4:]
    xb = out_ref.shape[0]
    cols, channels = out_ref.shape[-2:]
    tokens = xb * cols
    field = lambda which: items_ref[variant_ref[0], which, pl.program_id(0)]

    @pl.when(field(GROUP) == 0)
    def _():
        mixed_ref[...] = mine_ref[field(PLACE)]

    @pl.when(field(GROUP) == 1)
    def _():
        mixed_ref[...] = other_ref[field(PLACE)]

    start = field(BLOCK) * xb
    before, here, after = field(BEFORE), field(HERE), field(AFTER)
    taps = taps_ref[...]
    flip = field(FLIP) == 1
    tap_before = jnp.where(flip, taps[2:3], taps[0:1]).astype(BF16)
    tap_here = taps[1:2].astype(BF16)
    tap_after = jnp.where(flip, taps[0:1], taps[2:3])
    tap_after = jnp.where(field(DROP) == 1, 0.0, tap_after).astype(BF16)
    source = field(HALO)

    def load(row, s):
        return field_ref[pl.ds(start + s * sub // cols, sub // cols), row].reshape(sub, channels)

    def load_after(s):
        part = load(after, s)
        for at, ref in enumerate(halo_refs):
            halo = ref[s * sub // cols : (s + 1) * sub // cols].reshape(sub, channels)
            part = jnp.where(source == at + 1, halo, part)
        return part

    def join(s):
        rows = slice(s * sub, (s + 1) * sub)
        lines = pl.ds(pl.multiple_of(start * cols, xb * cols) + s * sub, sub)
        spectral = jnp.dot(inv_ref[lines], mixed_ref[...], preferred_element_type=F32)
        conv = (
            tap_before * load(before, s) + tap_here * load(here, s) + tap_after * load_after(s)
        )
        joined_ref[rows] = (spectral + conv.astype(F32)).astype(BF16)

    def expand(s):
        rows = slice(s * sub, (s + 1) * sub)
        x = jnp.dot(joined_ref[rows], w_in_ref[...], preferred_element_type=F32)
        x = (x + bias_in_ref[...]).astype(BF16)
        u = x * (BF16(GELU_A) + BF16(GELU_B) * (x * x))
        hidden_ref[rows] = x + x * jnp.tanh(u)

    def project(s):
        rows = slice(s * sub, (s + 1) * sub)
        y = jnp.dot(hidden_ref[rows], w_out_ref[...], preferred_element_type=F32)
        y = load(here, s).astype(F32) + (0.5 * y + bias_out_ref[...])
        out_ref[s * sub // cols : (s + 1) * sub // cols] = y.reshape(
            (sub // cols,) + out_ref.shape[1:]
        ).astype(BF16)

    parts = tokens // sub
    for s in range(parts + 2):
        if s < parts:
            join(s)
        if 0 <= s - 1 < parts:
            expand(s - 1)
        if s >= 2:
            project(s - 2)


def rows_of(out, field, inv, items, variant, taps, dense, mixed, halos, xb, sub):
    x_rows, y_rows, cols, channels = field.shape
    w_in, bias_in, w_out, bias_out = dense
    hidden = w_in.shape[1]
    waves_cols = inv.shape[1]
    count = items.shape[2]
    tokens = xb * cols
    args = [
        items, variant, field, inv, taps, w_in, bias_in, w_out, bias_out, *mixed, *halos,
    ]
    in_specs = [pl.BlockSpec(memory_space=pltpu.VMEM)] * (len(args) - 2)
    aliases = {}
    if out is not None:
        aliases = {len(args): 0}
        in_specs.append(pl.BlockSpec(memory_space=pl.ANY))
        args.append(out)
    return pl.pallas_call(
        functools.partial(row_kernel, len(halos), min(sub, tokens)),
        grid_spec=pltpu.PrefetchScalarGridSpec(
            num_scalar_prefetch=2,
            grid=(count,),
            in_specs=in_specs,
            out_specs=pl.BlockSpec(
                (xb, 1, cols, channels), lambda i, r, v: (r[v[0], BLOCK, i], r[v[0], HERE, i], 0, 0)
            ),
            scratch_shapes=[
                pltpu.VMEM((waves_cols, channels), BF16),
                pltpu.VMEM((tokens, channels), BF16),
                pltpu.VMEM((tokens, hidden), BF16),
            ],
        ),
        out_shape=jax.ShapeDtypeStruct(field.shape, BF16),
        input_output_aliases=aliases,
        compiler_params=pltpu.CompilerParams(vmem_limit_bytes=ROWS_BYTES),
        name="rows",
    )(*args)


def local(features, spectral_weight, conv_taps, w_in, bias_in, w_out, bias_out):
    x_rows, y_rows, cols, channels = features.shape
    modes = spectral_weight.shape[0]
    gx_size = lax.axis_size("gx")
    gy_size = lax.axis_size("gy")
    gx = lax.axis_index("gx")
    gy = lax.axis_index("gy")

    half_rows = y_rows // 2
    side = gx & 1
    variant = (gy % 2 * 2 + side).reshape(1)
    variants = [(odd, core) for odd in range(2) for core in range(2)]
    edges_of = lambda odd: [0 if odd else y_rows - 1, y_rows - 1 if odd else 0]
    live = [p for p in range(2) if gy_size > p + 1]
    side_rows = lambda core: [core * half_rows + i for i in range(half_rows)]
    order = jnp.array([side_rows(1 - core) + side_rows(core) for _, core in variants], jnp.int32)
    edge_rows = jnp.array([edges_of(odd) for odd, _ in variants], jnp.int32)

    levels = gx_size.bit_length() - 1
    halving = max(min(levels - 1, modes.bit_length()), 1)
    own = jnp.int32(0)
    for level in range(1, halving):
        own = own + (gx >> level & 1) * (modes >> level)
    table, inverse = wave_tables(own, gx * x_rows, modes, x_rows, x_rows * gx_size)
    swap = lambda a, level: lax.ppermute(
        a, "gx", [(i, i ^ (1 << level)) for i in range(gx_size)]
    )
    parts = half_rows
    xb = x_rows // parts
    halos = [[] for _ in range(parts)]
    send, keep = forward_transform(features, widen(table, cols), order, variant)
    owned = modes >> halving - 1
    inv, weight = prepare(inverse, cols, spectral_weight, own.reshape(1), owned)
    for level in range(levels):
        got = swap(send, level)
        cut = []
        if level < parts:
            for p in live:
                pairs = [(i, i + 1) for i in range(p, gy_size - 1, 2)]
                cut.append(cut_edge(features, edge_rows, variant, p, level, parts, send))
                halos[level].append(
                    lax.ppermute(cut[-1], "gy", pairs + [(b, a) for a, b in pairs])
                )
        if level + 1 < levels:
            ahead = cut + ([weight] if level == levels - 2 else [])
            send, keep = combine(keep, got, level + 1 < halving, ahead)
    mixed = mix(keep, got, weight)
    for level in reversed(range(2, halving)):
        mixed = join(mixed, swap(mixed, level))
    mixed = [stack_modes([mixed, swap(mixed, 1)] if halving > 1 else [mixed])]
    mixed.append(swap(mixed[0], 0))

    def block_of(core, before, here, after, part, halo=0, flip=0, drop=0):
        group = 0 if here // half_rows == core else 1
        return before, here, after, part, here % half_rows, group, halo, flip, drop

    def calls_of(odd, core):
        calls = [[] for _ in range(parts)]
        for row in range(1, y_rows - 1):
            for part in range(parts):
                calls[0].append(block_of(core, row - 1, row, row + 1, part))
        for p, edge in reversed(list(enumerate(edges_of(odd)))):
            inner, flip = (1, 1) if edge == 0 else (y_rows - 2, 0)
            for part in range(parts):
                halo = live.index(p) + 1 if p in live else 0
                calls[part if halo else 0].append(
                    block_of(core, inner, edge, edge, part, halo, flip, 0 if halo else 1)
                )
        return calls

    every = [calls_of(odd, core) for odd, core in variants]
    dense = (w_in, bias_in[None], w_out, bias_out[None])
    out = None
    for part in range(parts):
        items = jnp.array([list(zip(*calls[part])) for calls in every], jnp.int32)
        out = rows_of(
            out, features, inv, items, variant, conv_taps, dense, mixed, halos[part], xb, 512 if part == 0 else 256
        )
    return out


def solution(mesh):
    return jax.shard_map(
        local,
        mesh=mesh,
        in_specs=(P("gx", "gy", None, None), P(), P(), P(), P(), P(), P()),
        out_specs=P("gx", "gy", None, None),
        check_vma=False,
    )
```

```python
import functools
import math

import jax
import jax.numpy as jnp
from jax import lax
from jax.experimental import pallas as pl
from jax.experimental.pallas import tpu as pltpu
from jax.sharding import PartitionSpec as P

F32 = jnp.float32
BF16 = jnp.bfloat16
GELU_A = math.sqrt(2.0 / math.pi)
GELU_B = GELU_A * 0.044715
SMALL_BYTES = 16 * 2**20
ROWS_BYTES = 36 * 2**20


def wave_tables(own, start, modes, x_rows, total):
    shape = (2 * modes, x_rows)
    row = lax.broadcasted_iota(jnp.int32, shape, 0)
    waves = row // 2 ^ own
    product = waves * (start + lax.broadcasted_iota(jnp.int32, shape, 1)) % total
    angles = 2.0 * math.pi / total * product.astype(F32)
    scale = 1.0 / math.sqrt(total)
    parts = jnp.where(row % 2 == 0, jnp.cos(angles), -jnp.sin(angles))
    amplitude = jnp.where(waves == 0, 1.0, 2.0).astype(F32)
    return (parts * scale).astype(BF16), (amplitude * parts * scale).astype(BF16)


def spread(table, cols):
    waves, xb = table.shape
    columns = waves * cols
    place = (
        lax.broadcasted_iota(jnp.int32, (waves, columns), 1) // cols
        == lax.broadcasted_iota(jnp.int32, (waves, columns), 0)
    )
    tall = lax.dot_general(
        table, place.astype(F32).astype(BF16), (((0,), (0,)), ((), ())), preferred_element_type=F32
    )
    same = lax.broadcasted_iota(jnp.int32, (1, cols, columns), 2) % cols == lax.broadcasted_iota(
        jnp.int32, (1, cols, columns), 1
    )
    return jnp.where(same, tall[:, None, :], 0.0).reshape(xb * cols, columns).astype(BF16)


def spread_wide(table, cols):
    waves, xb = table.shape
    width = xb * cols
    place = (
        lax.broadcasted_iota(jnp.int32, (xb, width), 1) // cols
        == lax.broadcasted_iota(jnp.int32, (xb, width), 0)
    )
    wide = jnp.dot(table, place.astype(F32).astype(BF16), preferred_element_type=F32)
    same = lax.broadcasted_iota(jnp.int32, (1, cols, width), 2) % cols == lax.broadcasted_iota(
        jnp.int32, (1, cols, width), 1
    )
    return jnp.where(same, wide[:, None, :], 0.0).reshape(waves * cols, width).astype(BF16)


def widen_kernel(table_ref, wide_ref):
    x_rows = table_ref.shape[1]
    cols = wide_ref.shape[1] // x_rows
    xb = min(x_rows, 128)
    width = xb * cols
    for part in range(x_rows // xb):
        wide_ref[:, part * width : (part + 1) * width] = spread_wide(
            table_ref[:, part * xb : (part + 1) * xb], cols
        )


def widen(table, cols):
    waves, x_rows = table.shape
    return pl.pallas_call(
        widen_kernel,
        out_shape=jax.ShapeDtypeStruct((waves * cols, x_rows * cols), BF16),
        compiler_params=pltpu.CompilerParams(vmem_limit_bytes=SMALL_BYTES),
        cost_estimate=pl.CostEstimate(
            flops=5 * 10**9, bytes_accessed=4 * waves * cols * x_rows * cols, transcendentals=0
        ),
        name="widen",
    )(table)


def forward_kernel(live, place_ref, wide_ref, field_ref, send_ref, keep_ref, *edge_refs):
    x_rows, y_rows, cols, channels = field_ref.shape
    sent = send_ref.shape[1]
    waves = send_ref.shape[0]
    for place in range(y_rows):
        row = jnp.where(place_ref[0] >> 1 & 1 == 0, (place + sent) % y_rows, place)
        part = jnp.dot(
            wide_ref[...],
            field_ref[:, row].reshape(x_rows * cols, channels),
            preferred_element_type=F32,
        ).reshape(waves, cols, channels)
        if place < sent:
            send_ref[:, place] = part.astype(BF16)
        else:
            keep_ref[:, place - sent] = part
    odd = place_ref[0] & 1
    for p, ref in zip(live, edge_refs):
        ref[...] = field_ref[:, (odd if p else 1 - odd) * (y_rows - 1)]


def forward_transform(features, wide, place, live):
    x_rows, y_rows, cols, channels = features.shape
    shape = (wide.shape[0] // cols, y_rows // 2, cols, channels)
    vmem = pl.BlockSpec(memory_space=pltpu.VMEM)
    smem = pl.BlockSpec(memory_space=pltpu.SMEM)
    return pl.pallas_call(
        functools.partial(forward_kernel, live),
        in_specs=[smem, vmem, vmem],
        out_specs=[vmem] * (2 + len(live)),
        out_shape=[
            jax.ShapeDtypeStruct(shape, BF16),
            jax.ShapeDtypeStruct(shape, F32),
            *[jax.ShapeDtypeStruct((x_rows, cols, channels), BF16) for _ in live],
        ],
        compiler_params=pltpu.CompilerParams(vmem_limit_bytes=SMALL_BYTES),
        name="forward",
    )(place, wide, features)


def cut_kernel(start, edge_ref, ahead_ref, cut_ref):
    cut_ref[...] = edge_ref[start : start + cut_ref.shape[0]]


def cut_edge(edge, part, parts, ahead):
    count = edge.shape[0] // parts
    vmem = pl.BlockSpec(memory_space=pltpu.VMEM)
    return pl.pallas_call(
        functools.partial(cut_kernel, part * count),
        in_specs=[vmem, pl.BlockSpec(memory_space=pl.ANY)],
        out_specs=vmem,
        out_shape=jax.ShapeDtypeStruct((count,) + edge.shape[1:], BF16),
        compiler_params=pltpu.CompilerParams(vmem_limit_bytes=SMALL_BYTES),
        name="cut",
    )(edge, ahead)


def first_mode(gx, halving, modes):
    return sum((gx >> level & 1) * (modes >> level) for level in range(1, halving))


def prepare_kernel(halving, place_ref, table_ref, weight_ref, inv_ref, own_ref, sem):
    owned = own_ref.shape[0]
    first = first_mode(place_ref[0] >> 1, halving, weight_ref.shape[0])
    move = pltpu.make_async_copy(weight_ref.at[pl.ds(first, owned)], own_ref, sem)
    move.start()
    waves, x_rows = table_ref.shape
    cols = inv_ref.shape[0] // x_rows
    xb = min(x_rows, 128)
    for part in range(x_rows // xb):
        inv_ref[part * xb * cols : (part + 1) * xb * cols] = spread(
            table_ref[:, part * xb : (part + 1) * xb], cols
        )
    move.wait()


def prepare(table, cols, weight, place, halving):
    waves, x_rows = table.shape
    owned = weight.shape[0] >> halving - 1
    vmem = pl.BlockSpec(memory_space=pltpu.VMEM)
    return pl.pallas_call(
        functools.partial(prepare_kernel, halving),
        in_specs=[
            pl.BlockSpec(memory_space=pltpu.SMEM),
            vmem,
            pl.BlockSpec(memory_space=pltpu.HBM),
        ],
        out_specs=[vmem, vmem],
        out_shape=[
            jax.ShapeDtypeStruct((x_rows * cols, waves * cols), BF16),
            jax.ShapeDtypeStruct((owned,) + weight.shape[1:], BF16),
        ],
        scratch_shapes=[pltpu.SemaphoreType.DMA],
        compiler_params=pltpu.CompilerParams(vmem_limit_bytes=SMALL_BYTES),
        name="prepare",
    )(place, table, weight)


def halve_kernel(half, keep_ref, got_ref, *refs):
    send_ref, next_ref = refs[-2:]
    next_ref[...] = keep_ref[:half] + got_ref[:half].astype(F32)
    send_ref[...] = (keep_ref[half:] + got_ref[half:].astype(F32)).astype(BF16)


def add_kernel(keep_ref, got_ref, *refs):
    send_ref, next_ref = refs[-2:]
    total = keep_ref[...] + got_ref[...].astype(F32)
    next_ref[...] = total
    send_ref[...] = total.astype(BF16)


def combine(keep, got, halve, ahead):
    half = keep.shape[0] // 2 if halve else keep.shape[0]
    shape = (half,) + keep.shape[1:]
    vmem = pl.BlockSpec(memory_space=pltpu.VMEM)
    return pl.pallas_call(
        functools.partial(halve_kernel, half) if halve else add_kernel,
        in_specs=[vmem, vmem] + [pl.BlockSpec(memory_space=pl.ANY)] * len(ahead),
        out_specs=[vmem, vmem],
        out_shape=[jax.ShapeDtypeStruct(shape, BF16), jax.ShapeDtypeStruct(shape, F32)],
        compiler_params=pltpu.CompilerParams(vmem_limit_bytes=SMALL_BYTES),
        name="halve" if halve else "add",
    )(keep, got, *ahead)


def join_kernel(mine_ref, got_ref, out_ref):
    half = mine_ref.shape[0]
    out_ref[:half] = mine_ref[...]
    out_ref[half:] = got_ref[...]


def join(mine, got):
    return pl.pallas_call(
        join_kernel,
        out_shape=jax.ShapeDtypeStruct((2 * mine.shape[0],) + mine.shape[1:], BF16),
        compiler_params=pltpu.CompilerParams(vmem_limit_bytes=SMALL_BYTES),
        name="join",
    )(mine, got)


def stack_kernel(*refs):
    out_ref = refs[-1]
    rows, _, channels = out_ref.shape
    at = 0
    for ref in refs[:-1]:
        count = ref.shape[0] * ref.shape[2]
        for row in range(rows):
            out_ref[row, at : at + count] = ref[:, row].reshape(count, channels)
        at += count


def stack_modes(pieces):
    waves = sum(p.shape[0] for p in pieces)
    _, rows, cols, channels = pieces[0].shape
    return pl.pallas_call(
        stack_kernel,
        out_shape=jax.ShapeDtypeStruct((rows, waves * cols, channels), BF16),
        compiler_params=pltpu.CompilerParams(vmem_limit_bytes=SMALL_BYTES),
        name="stack",
    )(*pieces)


def mix_kernel(keep_ref, got_ref, weight_ref, out_ref):
    modes = weight_ref.shape[0]
    _, rows, cols, channels = keep_ref.shape
    count = rows * cols
    dot = functools.partial(jnp.dot, preferred_element_type=F32)
    for mode in range(modes):
        both = slice(2 * mode, 2 * mode + 2)
        parts = keep_ref[both] + got_ref[both].astype(F32)
        parts = parts.reshape(2 * count, channels).astype(BF16)
        by_real = dot(parts, weight_ref[mode, 0])
        by_imag = dot(parts, weight_ref[mode, 1])
        mixed_real = by_real[:count] - by_imag[count:]
        mixed_imag = by_imag[:count] + by_real[count:]
        out_ref[2 * mode] = mixed_real.reshape(rows, cols, channels).astype(BF16)
        out_ref[2 * mode + 1] = mixed_imag.reshape(rows, cols, channels).astype(BF16)


def mix(keep, got, weight):
    return pl.pallas_call(
        mix_kernel,
        out_shape=jax.ShapeDtypeStruct(keep.shape, BF16),
        compiler_params=pltpu.CompilerParams(vmem_limit_bytes=SMALL_BYTES),
        name="mix",
    )(keep, got, weight)


BEFORE, HERE, AFTER, BLOCK, PLACE, GROUP, HALO, FLIP, DROP = range(9)


def row_kernel(
    halos, sub, items_ref, place_ref, field_ref, inv_ref, taps_ref,
    w_in_ref, bias_in_ref, w_out_ref, bias_out_ref, mine_ref, other_ref, *rest
):
    halo_refs = rest[:halos]
    out_ref, mixed_ref, joined_ref, hidden_ref = rest[-4:]
    xb = out_ref.shape[0]
    cols, channels = out_ref.shape[-2:]
    tokens = xb * cols
    field = lambda which: items_ref[place_ref[0] & 3, which, pl.program_id(0)]

    @pl.when(field(GROUP) == 0)
    def _():
        mixed_ref[...] = mine_ref[field(PLACE)]

    @pl.when(field(GROUP) == 1)
    def _():
        mixed_ref[...] = other_ref[field(PLACE)]

    start = field(BLOCK) * xb
    before, here, after = field(BEFORE), field(HERE), field(AFTER)
    taps = taps_ref[...]
    flip = field(FLIP) == 1
    tap_before = jnp.where(flip, taps[2:3], taps[0:1]).astype(BF16)
    tap_here = taps[1:2].astype(BF16)
    tap_after = jnp.where(flip, taps[0:1], taps[2:3])
    tap_after = jnp.where(field(DROP) == 1, 0.0, tap_after).astype(BF16)
    source = field(HALO)

    def load(row, s):
        return field_ref[pl.ds(start + s * sub // cols, sub // cols), row].reshape(sub, channels)

    def load_after(s):
        part = load(after, s)
        for at, ref in enumerate(halo_refs):
            halo = ref[s * sub // cols : (s + 1) * sub // cols].reshape(sub, channels)
            part = jnp.where(source == at + 1, halo, part)
        return part

    def join(s):
        rows = slice(s * sub, (s + 1) * sub)
        lines = pl.ds(pl.multiple_of(start * cols, xb * cols) + s * sub, sub)
        spectral = jnp.dot(inv_ref[lines], mixed_ref[...], preferred_element_type=F32)
        conv = (
            tap_before * load(before, s) + tap_here * load(here, s) + tap_after * load_after(s)
        )
        joined_ref[rows] = (spectral + conv.astype(F32)).astype(BF16)

    def expand(s):
        rows = slice(s * sub, (s + 1) * sub)
        x = jnp.dot(joined_ref[rows], w_in_ref[...], preferred_element_type=F32)
        x = (x + bias_in_ref[...]).astype(BF16)
        u = x * (BF16(GELU_A) + BF16(GELU_B) * (x * x))
        hidden_ref[rows] = x + x * jnp.tanh(u)

    def project(s):
        rows = slice(s * sub, (s + 1) * sub)
        y = jnp.dot(hidden_ref[rows], w_out_ref[...], preferred_element_type=F32)
        y = load(here, s).astype(F32) + (0.5 * y + bias_out_ref[...])
        out_ref[s * sub // cols : (s + 1) * sub // cols] = y.reshape(
            (sub // cols,) + out_ref.shape[1:]
        ).astype(BF16)

    parts = tokens // sub
    for s in range(parts + 2):
        if s < parts:
            join(s)
        if 0 <= s - 1 < parts:
            expand(s - 1)
        if s >= 2:
            project(s - 2)


def rows_of(out, field, inv, items, place, taps, dense, mixed, halos, xb, sub):
    x_rows, y_rows, cols, channels = field.shape
    w_in, bias_in, w_out, bias_out = dense
    hidden = w_in.shape[1]
    waves_cols = inv.shape[1]
    count = items.shape[2]
    tokens = xb * cols
    args = [
        items, place, field, inv, taps, w_in, bias_in, w_out, bias_out, *mixed, *halos,
    ]
    in_specs = [pl.BlockSpec(memory_space=pltpu.VMEM)] * (len(args) - 2)
    aliases = {}
    if out is not None:
        aliases = {len(args): 0}
        in_specs.append(pl.BlockSpec(memory_space=pl.ANY))
        args.append(out)
    return pl.pallas_call(
        functools.partial(row_kernel, len(halos), min(sub, tokens)),
        grid_spec=pltpu.PrefetchScalarGridSpec(
            num_scalar_prefetch=2,
            grid=(count,),
            in_specs=in_specs,
            out_specs=pl.BlockSpec(
                (xb, 1, cols, channels), lambda i, r, v: (r[v[0] & 3, BLOCK, i], r[v[0] & 3, HERE, i], 0, 0)
            ),
            scratch_shapes=[
                pltpu.VMEM((waves_cols, channels), BF16),
                pltpu.VMEM((tokens, channels), BF16),
                pltpu.VMEM((tokens, hidden), BF16),
            ],
        ),
        out_shape=jax.ShapeDtypeStruct(field.shape, BF16),
        input_output_aliases=aliases,
        compiler_params=pltpu.CompilerParams(vmem_limit_bytes=ROWS_BYTES),
        name="rows",
    )(*args)


def local(features, spectral_weight, conv_taps, w_in, bias_in, w_out, bias_out):
    x_rows, y_rows, cols, channels = features.shape
    modes = spectral_weight.shape[0]
    gx_size = lax.axis_size("gx")
    gy_size = lax.axis_size("gy")
    gx = lax.axis_index("gx")
    gy = lax.axis_index("gy")

    half_rows = y_rows // 2
    place = (gx * 2 + gy % 2).reshape(1)
    variants = [(odd, core) for core in range(2) for odd in range(2)]
    edges_of = lambda odd: [0 if odd else y_rows - 1, y_rows - 1 if odd else 0]
    live = [p for p in range(2) if gy_size > p + 1]

    levels = gx_size.bit_length() - 1
    halving = max(min(levels - 1, modes.bit_length()), 1)
    own = first_mode(gx, halving, modes)
    table, inverse = wave_tables(own, gx * x_rows, modes, x_rows, x_rows * gx_size)
    swap = lambda a, level: lax.ppermute(
        a, "gx", [(i, i ^ (1 << level)) for i in range(gx_size)]
    )
    parts = half_rows
    xb = x_rows // parts
    halos = [[] for _ in range(parts)]
    send, keep, *edge = forward_transform(features, widen(table, cols), place, live)
    inv, weight = prepare(inverse, cols, spectral_weight, place, halving)
    for level in range(levels):
        got = swap(send, level)
        cut = []
        if level < parts:
            for p in live:
                pairs = [(i, i + 1) for i in range(p, gy_size - 1, 2)]
                cut.append(cut_edge(edge[live.index(p)], level, parts, send))
                halos[level].append(
                    lax.ppermute(cut[-1], "gy", pairs + [(b, a) for a, b in pairs])
                )
        if level + 1 < levels:
            ahead = cut + ([weight] if level == levels - 2 else [])
            send, keep = combine(keep, got, level + 1 < halving, ahead)
    mixed = mix(keep, got, weight)
    for level in reversed(range(2, halving)):
        mixed = join(mixed, swap(mixed, level))
    mixed = [stack_modes([mixed, swap(mixed, 1)] if halving > 1 else [mixed])]
    mixed.append(swap(mixed[0], 0))

    def block_of(core, before, here, after, part, halo=0, flip=0, drop=0):
        group = 0 if here // half_rows == core else 1
        return before, here, after, part, here % half_rows, group, halo, flip, drop

    def calls_of(odd, core):
        calls = [[] for _ in range(parts)]
        for row in range(1, y_rows - 1):
            for part in range(parts):
                calls[0].append(block_of(core, row - 1, row, row + 1, part))
        for p, edge in reversed(list(enumerate(edges_of(odd)))):
            inner, flip = (1, 1) if edge == 0 else (y_rows - 2, 0)
            for part in range(parts):
                halo = live.index(p) + 1 if p in live else 0
                calls[part if halo else 0].append(
                    block_of(core, inner, edge, edge, part, halo, flip, 0 if halo else 1)
                )
        return calls

    every = [calls_of(odd, core) for odd, core in variants]
    dense = (w_in, bias_in[None], w_out, bias_out[None])
    out = None
    for part in range(parts):
        items = jnp.array([list(zip(*calls[part])) for calls in every], jnp.int32)
        out = rows_of(
            out, features, inv, items, place, conv_taps, dense, mixed, halos[part], xb, 512
        )
    return out


def solution(mesh):
    return jax.shard_map(
        local,
        mesh=mesh,
        in_specs=(P("gx", "gy", None, None), P(), P(), P(), P(), P(), P()),
        out_specs=P("gx", "gy", None, None),
        check_vma=False,
    )
```

```python
import functools
import math

import jax
import jax.numpy as jnp
from jax import lax
from jax.experimental import pallas as pl
from jax.experimental.pallas import tpu as pltpu
from jax.sharding import PartitionSpec as P

F32 = jnp.float32
BF16 = jnp.bfloat16
GELU_A = math.sqrt(2.0 / math.pi)
GELU_B = GELU_A * 0.044715
SMALL_BYTES = 16 * 2**20
ROWS_BYTES = 36 * 2**20


def wave_tables(own, start, modes, x_rows, total):
    shape = (2 * modes, x_rows)
    row = lax.broadcasted_iota(jnp.int32, shape, 0)
    waves = row // 2 ^ own
    product = waves * (start + lax.broadcasted_iota(jnp.int32, shape, 1)) % total
    angles = 2.0 * math.pi / total * product.astype(F32)
    scale = 1.0 / math.sqrt(total)
    parts = jnp.where(row % 2 == 0, jnp.cos(angles), -jnp.sin(angles))
    amplitude = jnp.where(waves == 0, 1.0, 2.0).astype(F32)
    return (parts * scale).astype(BF16), (amplitude * parts * scale).astype(BF16)


def spread(table, cols):
    waves, xb = table.shape
    columns = waves * cols
    place = (
        lax.broadcasted_iota(jnp.int32, (waves, columns), 1) // cols
        == lax.broadcasted_iota(jnp.int32, (waves, columns), 0)
    )
    tall = lax.dot_general(
        table, place.astype(F32).astype(BF16), (((0,), (0,)), ((), ())), preferred_element_type=F32
    )
    same = lax.broadcasted_iota(jnp.int32, (1, cols, columns), 2) % cols == lax.broadcasted_iota(
        jnp.int32, (1, cols, columns), 1
    )
    return jnp.where(same, tall[:, None, :], 0.0).reshape(xb * cols, columns).astype(BF16)


def spread_wide(table, cols):
    waves, xb = table.shape
    width = xb * cols
    place = (
        lax.broadcasted_iota(jnp.int32, (xb, width), 1) // cols
        == lax.broadcasted_iota(jnp.int32, (xb, width), 0)
    )
    wide = jnp.dot(table, place.astype(F32).astype(BF16), preferred_element_type=F32)
    same = lax.broadcasted_iota(jnp.int32, (1, cols, width), 2) % cols == lax.broadcasted_iota(
        jnp.int32, (1, cols, width), 1
    )
    return jnp.where(same, wide[:, None, :], 0.0).reshape(waves * cols, width).astype(BF16)


def widen_kernel(table_ref, wide_ref):
    x_rows = table_ref.shape[1]
    cols = wide_ref.shape[1] // x_rows
    xb = min(x_rows, 128)
    width = xb * cols
    for part in range(x_rows // xb):
        wide_ref[:, part * width : (part + 1) * width] = spread_wide(
            table_ref[:, part * xb : (part + 1) * xb], cols
        )


def widen(table, cols):
    waves, x_rows = table.shape
    return pl.pallas_call(
        widen_kernel,
        out_shape=jax.ShapeDtypeStruct((waves * cols, x_rows * cols), BF16),
        compiler_params=pltpu.CompilerParams(vmem_limit_bytes=SMALL_BYTES),
        cost_estimate=pl.CostEstimate(
            flops=5 * 10**9, bytes_accessed=4 * waves * cols * x_rows * cols, transcendentals=0
        ),
        name="widen",
    )(table)


def forward_kernel(live, place_ref, wide_ref, field_ref, send_ref, keep_ref, *edge_refs):
    x_rows, y_rows, cols, channels = field_ref.shape
    sent = send_ref.shape[1]
    waves = send_ref.shape[0]
    for place in range(y_rows):
        row = jnp.where(place_ref[0] >> 1 & 1 == 0, (place + sent) % y_rows, place)
        part = jnp.dot(
            wide_ref[...],
            field_ref[:, row].reshape(x_rows * cols, channels),
            preferred_element_type=F32,
        ).reshape(waves, cols, channels)
        if place < sent:
            send_ref[:, place] = part.astype(BF16)
        else:
            keep_ref[:, place - sent] = part
    odd = place_ref[0] & 1
    for p, ref in zip(live, edge_refs):
        ref[...] = field_ref[:, (odd if p else 1 - odd) * (y_rows - 1)]


def forward_transform(features, wide, place, live):
    x_rows, y_rows, cols, channels = features.shape
    shape = (wide.shape[0] // cols, y_rows // 2, cols, channels)
    vmem = pl.BlockSpec(memory_space=pltpu.VMEM)
    smem = pl.BlockSpec(memory_space=pltpu.SMEM)
    return pl.pallas_call(
        functools.partial(forward_kernel, live),
        in_specs=[smem, vmem, vmem],
        out_specs=[vmem] * (2 + len(live)),
        out_shape=[
            jax.ShapeDtypeStruct(shape, BF16),
            jax.ShapeDtypeStruct(shape, F32),
            *[jax.ShapeDtypeStruct((x_rows, cols, channels), BF16) for _ in live],
        ],
        compiler_params=pltpu.CompilerParams(vmem_limit_bytes=SMALL_BYTES),
        name="forward",
    )(place, wide, features)


def hold_kernel(edge_ref, ahead_ref, out_ref):
    out_ref[...] = edge_ref[...]


def hold(edge, ahead):
    vmem = pl.BlockSpec(memory_space=pltpu.VMEM)
    return pl.pallas_call(
        hold_kernel,
        in_specs=[vmem, pl.BlockSpec(memory_space=pl.ANY)],
        out_specs=vmem,
        out_shape=jax.ShapeDtypeStruct(edge.shape, BF16),
        compiler_params=pltpu.CompilerParams(vmem_limit_bytes=SMALL_BYTES),
        name="hold",
    )(edge, ahead)


def first_mode(gx, halving, modes):
    return sum((gx >> level & 1) * (modes >> level) for level in range(1, halving))


def prepare_kernel(halving, place_ref, table_ref, weight_ref, inv_ref, own_ref, sem):
    owned = own_ref.shape[0]
    first = first_mode(place_ref[0] >> 1, halving, weight_ref.shape[0])
    move = pltpu.make_async_copy(weight_ref.at[pl.ds(first, owned)], own_ref, sem)
    move.start()
    waves, x_rows = table_ref.shape
    cols = inv_ref.shape[0] // x_rows
    xb = min(x_rows, 128)
    for part in range(x_rows // xb):
        inv_ref[part * xb * cols : (part + 1) * xb * cols] = spread(
            table_ref[:, part * xb : (part + 1) * xb], cols
        )
    move.wait()


def prepare(table, cols, weight, place, halving):
    waves, x_rows = table.shape
    owned = weight.shape[0] >> halving - 1
    vmem = pl.BlockSpec(memory_space=pltpu.VMEM)
    return pl.pallas_call(
        functools.partial(prepare_kernel, halving),
        in_specs=[
            pl.BlockSpec(memory_space=pltpu.SMEM),
            vmem,
            pl.BlockSpec(memory_space=pltpu.HBM),
        ],
        out_specs=[vmem, vmem],
        out_shape=[
            jax.ShapeDtypeStruct((x_rows * cols, waves * cols), BF16),
            jax.ShapeDtypeStruct((owned,) + weight.shape[1:], BF16),
        ],
        scratch_shapes=[pltpu.SemaphoreType.DMA],
        compiler_params=pltpu.CompilerParams(vmem_limit_bytes=SMALL_BYTES),
        name="prepare",
    )(place, table, weight)


def halve_kernel(half, keep_ref, got_ref, *refs):
    send_ref, next_ref = refs[-2:]
    next_ref[...] = keep_ref[:half] + got_ref[:half].astype(F32)
    send_ref[...] = (keep_ref[half:] + got_ref[half:].astype(F32)).astype(BF16)


def add_kernel(keep_ref, got_ref, *refs):
    send_ref, next_ref = refs[-2:]
    total = keep_ref[...] + got_ref[...].astype(F32)
    next_ref[...] = total
    send_ref[...] = total.astype(BF16)


def combine(keep, got, halve, ahead):
    half = keep.shape[0] // 2 if halve else keep.shape[0]
    shape = (half,) + keep.shape[1:]
    vmem = pl.BlockSpec(memory_space=pltpu.VMEM)
    return pl.pallas_call(
        functools.partial(halve_kernel, half) if halve else add_kernel,
        in_specs=[vmem, vmem] + [pl.BlockSpec(memory_space=pl.ANY)] * len(ahead),
        out_specs=[vmem, vmem],
        out_shape=[jax.ShapeDtypeStruct(shape, BF16), jax.ShapeDtypeStruct(shape, F32)],
        compiler_params=pltpu.CompilerParams(vmem_limit_bytes=SMALL_BYTES),
        name="halve" if halve else "add",
    )(keep, got, *ahead)


def join_kernel(mine_ref, got_ref, out_ref):
    half = mine_ref.shape[0]
    out_ref[:half] = mine_ref[...]
    out_ref[half:] = got_ref[...]


def join(mine, got):
    return pl.pallas_call(
        join_kernel,
        out_shape=jax.ShapeDtypeStruct((2 * mine.shape[0],) + mine.shape[1:], BF16),
        compiler_params=pltpu.CompilerParams(vmem_limit_bytes=SMALL_BYTES),
        name="join",
    )(mine, got)


def stack_kernel(*refs):
    out_ref = refs[-1]
    rows, _, channels = out_ref.shape
    at = 0
    for ref in refs[:-1]:
        count = ref.shape[0] * ref.shape[2]
        for row in range(rows):
            out_ref[row, at : at + count] = ref[:, row].reshape(count, channels)
        at += count


def stack_modes(pieces):
    waves = sum(p.shape[0] for p in pieces)
    _, rows, cols, channels = pieces[0].shape
    return pl.pallas_call(
        stack_kernel,
        out_shape=jax.ShapeDtypeStruct((rows, waves * cols, channels), BF16),
        compiler_params=pltpu.CompilerParams(vmem_limit_bytes=SMALL_BYTES),
        name="stack",
    )(*pieces)


def mix_kernel(keep_ref, got_ref, weight_ref, out_ref):
    modes = weight_ref.shape[0]
    _, rows, cols, channels = keep_ref.shape
    count = rows * cols
    dot = functools.partial(jnp.dot, preferred_element_type=F32)
    for mode in range(modes):
        both = slice(2 * mode, 2 * mode + 2)
        parts = keep_ref[both] + got_ref[both].astype(F32)
        parts = parts.reshape(2 * count, channels).astype(BF16)
        by_real = dot(parts, weight_ref[mode, 0])
        by_imag = dot(parts, weight_ref[mode, 1])
        mixed_real = by_real[:count] - by_imag[count:]
        mixed_imag = by_imag[:count] + by_real[count:]
        out_ref[2 * mode] = mixed_real.reshape(rows, cols, channels).astype(BF16)
        out_ref[2 * mode + 1] = mixed_imag.reshape(rows, cols, channels).astype(BF16)


def mix(keep, got, weight):
    return pl.pallas_call(
        mix_kernel,
        out_shape=jax.ShapeDtypeStruct(keep.shape, BF16),
        compiler_params=pltpu.CompilerParams(vmem_limit_bytes=SMALL_BYTES),
        name="mix",
    )(keep, got, weight)


BEFORE, HERE, AFTER, BLOCK, PLACE, GROUP, HALO, FLIP, DROP = range(9)


def row_kernel(
    halos, sub, items_ref, place_ref, field_ref, inv_ref, taps_ref,
    w_in_ref, bias_in_ref, w_out_ref, bias_out_ref, mine_ref, other_ref, *rest
):
    halo_refs = rest[:halos]
    out_ref, mixed_ref, joined_ref, hidden_ref = rest[-4:]
    xb = out_ref.shape[0]
    cols, channels = out_ref.shape[-2:]
    tokens = xb * cols
    field = lambda which: items_ref[place_ref[0] & 3, which, pl.program_id(0)]

    @pl.when(field(GROUP) == 0)
    def _():
        mixed_ref[...] = mine_ref[field(PLACE)]

    @pl.when(field(GROUP) == 1)
    def _():
        mixed_ref[...] = other_ref[field(PLACE)]

    start = field(BLOCK) * xb
    before, here, after = field(BEFORE), field(HERE), field(AFTER)
    taps = taps_ref[...]
    flip = field(FLIP) == 1
    tap_before = jnp.where(flip, taps[2:3], taps[0:1]).astype(BF16)
    tap_here = taps[1:2].astype(BF16)
    tap_after = jnp.where(flip, taps[0:1], taps[2:3])
    tap_after = jnp.where(field(DROP) == 1, 0.0, tap_after).astype(BF16)
    source = field(HALO)

    def load(row, s):
        return field_ref[pl.ds(start + s * sub // cols, sub // cols), row].reshape(sub, channels)

    def load_after(s):
        part = load(after, s)
        for at, ref in enumerate(halo_refs):
            halo = ref[pl.ds(start + s * sub // cols, sub // cols)].reshape(sub, channels)
            part = jnp.where(source == at + 1, halo, part)
        return part

    def join(s):
        rows = slice(s * sub, (s + 1) * sub)
        lines = pl.ds(pl.multiple_of(start * cols, xb * cols) + s * sub, sub)
        spectral = jnp.dot(inv_ref[lines], mixed_ref[...], preferred_element_type=F32)
        conv = (
            tap_before * load(before, s) + tap_here * load(here, s) + tap_after * load_after(s)
        )
        joined_ref[rows] = (spectral + conv.astype(F32)).astype(BF16)

    def expand(s):
        rows = slice(s * sub, (s + 1) * sub)
        x = jnp.dot(joined_ref[rows], w_in_ref[...], preferred_element_type=F32)
        x = (x + bias_in_ref[...]).astype(BF16)
        u = x * (BF16(GELU_A) + BF16(GELU_B) * (x * x))
        hidden_ref[rows] = x + x * jnp.tanh(u)

    def project(s):
        rows = slice(s * sub, (s + 1) * sub)
        y = jnp.dot(hidden_ref[rows], w_out_ref[...], preferred_element_type=F32)
        y = load(here, s).astype(F32) + (0.5 * y + bias_out_ref[...])
        out_ref[s * sub // cols : (s + 1) * sub // cols] = y.reshape(
            (sub // cols,) + out_ref.shape[1:]
        ).astype(BF16)

    parts = tokens // sub
    for s in range(parts + 2):
        if s < parts:
            join(s)
        if 0 <= s - 1 < parts:
            expand(s - 1)
        if s >= 2:
            project(s - 2)


def rows_of(out, field, inv, items, place, taps, dense, mixed, halos, xb, sub):
    x_rows, y_rows, cols, channels = field.shape
    w_in, bias_in, w_out, bias_out = dense
    hidden = w_in.shape[1]
    waves_cols = inv.shape[1]
    count = items.shape[2]
    tokens = xb * cols
    args = [
        items, place, field, inv, taps, w_in, bias_in, w_out, bias_out, *mixed, *halos,
    ]
    in_specs = [pl.BlockSpec(memory_space=pltpu.VMEM)] * (len(args) - 2)
    aliases = {}
    if out is not None:
        aliases = {len(args): 0}
        in_specs.append(pl.BlockSpec(memory_space=pl.ANY))
        args.append(out)
    return pl.pallas_call(
        functools.partial(row_kernel, len(halos), min(sub, tokens)),
        grid_spec=pltpu.PrefetchScalarGridSpec(
            num_scalar_prefetch=2,
            grid=(count,),
            in_specs=in_specs,
            out_specs=pl.BlockSpec(
                (xb, 1, cols, channels), lambda i, r, v: (r[v[0] & 3, BLOCK, i], r[v[0] & 3, HERE, i], 0, 0)
            ),
            scratch_shapes=[
                pltpu.VMEM((waves_cols, channels), BF16),
                pltpu.VMEM((tokens, channels), BF16),
                pltpu.VMEM((tokens, hidden), BF16),
            ],
        ),
        out_shape=jax.ShapeDtypeStruct(field.shape, BF16),
        input_output_aliases=aliases,
        compiler_params=pltpu.CompilerParams(vmem_limit_bytes=ROWS_BYTES),
        cost_estimate=pl.CostEstimate(
            flops=2 * count * tokens * channels * (2 * hidden + waves_cols),
            bytes_accessed=2 * count * tokens * channels,
            transcendentals=count * tokens * hidden,
        ),
        name="rows",
    )(*args)


def local(features, spectral_weight, conv_taps, w_in, bias_in, w_out, bias_out):
    x_rows, y_rows, cols, channels = features.shape
    modes = spectral_weight.shape[0]
    gx_size = lax.axis_size("gx")
    gy_size = lax.axis_size("gy")
    gx = lax.axis_index("gx")
    gy = lax.axis_index("gy")

    half_rows = y_rows // 2
    place = (gx * 2 + gy % 2).reshape(1)
    variants = [(odd, core) for core in range(2) for odd in range(2)]
    edges_of = lambda odd: [0 if odd else y_rows - 1, y_rows - 1 if odd else 0]
    live = [p for p in range(2) if gy_size > p + 1]

    levels = gx_size.bit_length() - 1
    halving = max(min(levels - 1, modes.bit_length()), 1)
    own = first_mode(gx, halving, modes)
    table, inverse = wave_tables(own, gx * x_rows, modes, x_rows, x_rows * gx_size)
    swap = lambda a, level: lax.ppermute(
        a, "gx", [(i, i ^ (1 << level)) for i in range(gx_size)]
    )
    parts = half_rows
    xb = x_rows // parts
    halos = []
    send, keep, *edge = forward_transform(features, widen(table, cols), place, live)
    inv, weight = prepare(inverse, cols, spectral_weight, place, halving)
    for level in range(levels):
        got = swap(send, level)
        ahead = []
        if level == 0:
            for p, row in zip(live, edge):
                pairs = [(i, i + 1) for i in range(p, gy_size - 1, 2)]
                ahead.append(hold(row, send))
                halos.append(lax.ppermute(ahead[-1], "gy", pairs + [(b, a) for a, b in pairs]))
        if level + 1 < levels:
            ahead += [weight] if level == levels - 2 else []
            send, keep = combine(keep, got, level + 1 < halving, ahead)
    mixed = mix(keep, got, weight)
    for level in reversed(range(2, halving)):
        mixed = join(mixed, swap(mixed, level))
    mixed = [stack_modes([mixed, swap(mixed, 1)] if halving > 1 else [mixed])]
    mixed.append(swap(mixed[0], 0))

    def block_of(core, before, here, after, part, halo=0, flip=0, drop=0):
        group = 0 if here // half_rows == core else 1
        return before, here, after, part, here % half_rows, group, halo, flip, drop

    def calls_of(odd, core):
        calls = [[], []]
        for row in range(1, y_rows - 1):
            for part in range(parts):
                calls[0].append(block_of(core, row - 1, row, row + 1, part))
        for p, edge in reversed(list(enumerate(edges_of(odd)))):
            inner, flip = (1, 1) if edge == 0 else (y_rows - 2, 0)
            for part in range(parts):
                halo = live.index(p) + 1 if p in live else 0
                calls[1 if halo else 0].append(
                    block_of(core, inner, edge, edge, part, halo, flip, 0 if halo else 1)
                )
        return calls

    every = [calls_of(odd, core) for odd, core in variants]
    dense = (w_in, bias_in[None], w_out, bias_out[None])
    out = None
    for call in range(2 if live else 1):
        items = jnp.array([list(zip(*calls[call])) for calls in every], jnp.int32)
        out = rows_of(
            out, features, inv, items, place, conv_taps, dense, mixed, halos if call else [], xb, 512
        )
    return out


def solution(mesh):
    return jax.shard_map(
        local,
        mesh=mesh,
        in_specs=(P("gx", "gy", None, None), P(), P(), P(), P(), P(), P()),
        out_specs=P("gx", "gy", None, None),
        check_vma=False,
    )
```

```python
import functools
import math

import jax
import jax.numpy as jnp
from jax import lax
from jax.experimental import pallas as pl
from jax.experimental.pallas import tpu as pltpu
from jax.sharding import PartitionSpec as P

F32 = jnp.float32
BF16 = jnp.bfloat16
GELU_A = math.sqrt(2.0 / math.pi)
GELU_B = GELU_A * 0.044715
SMALL_BYTES = 16 * 2**20
ROWS_BYTES = 36 * 2**20


def wave_table(gx, halving, modes, x_rows, total, inverse):
    shape = (2 * modes, x_rows)
    row = lax.broadcasted_iota(jnp.int32, shape, 0)
    waves = row // 2 ^ first_mode(gx, halving, modes)
    product = waves * (gx * x_rows + lax.broadcasted_iota(jnp.int32, shape, 1)) % total
    angles = 2.0 * math.pi / total * product.astype(F32)
    parts = jnp.where(row % 2 == 0, jnp.cos(angles), -jnp.sin(angles))
    if inverse:
        parts = jnp.where(waves == 0, 1.0, 2.0) * parts
    return (parts * (1.0 / math.sqrt(total))).astype(BF16)


def spread(table, cols):
    waves, xb = table.shape
    columns = waves * cols
    place = (
        lax.broadcasted_iota(jnp.int32, (waves, columns), 1) // cols
        == lax.broadcasted_iota(jnp.int32, (waves, columns), 0)
    )
    tall = lax.dot_general(
        table, place.astype(F32).astype(BF16), (((0,), (0,)), ((), ())), preferred_element_type=F32
    )
    same = lax.broadcasted_iota(jnp.int32, (1, cols, columns), 2) % cols == lax.broadcasted_iota(
        jnp.int32, (1, cols, columns), 1
    )
    return jnp.where(same, tall[:, None, :], 0.0).reshape(xb * cols, columns).astype(BF16)


def spread_wide(table, cols):
    waves, xb = table.shape
    width = xb * cols
    place = (
        lax.broadcasted_iota(jnp.int32, (xb, width), 1) // cols
        == lax.broadcasted_iota(jnp.int32, (xb, width), 0)
    )
    wide = jnp.dot(table, place.astype(F32).astype(BF16), preferred_element_type=F32)
    same = lax.broadcasted_iota(jnp.int32, (1, cols, width), 2) % cols == lax.broadcasted_iota(
        jnp.int32, (1, cols, width), 1
    )
    return jnp.where(same, wide[:, None, :], 0.0).reshape(waves * cols, width).astype(BF16)


def widen_kernel(halving, modes, total, place_ref, wide_ref):
    cols = wide_ref.shape[0] // (2 * modes)
    x_rows = wide_ref.shape[1] // cols
    table = wave_table(place_ref[0] >> 1, halving, modes, x_rows, total, False)
    xb = min(x_rows, 128)
    width = xb * cols
    for part in range(x_rows // xb):
        wide_ref[:, part * width : (part + 1) * width] = spread_wide(
            table[:, part * xb : (part + 1) * xb], cols
        )


def widen(place, halving, modes, cols, x_rows, total):
    rows = 2 * modes
    return pl.pallas_call(
        functools.partial(widen_kernel, halving, modes, total),
        in_specs=[pl.BlockSpec(memory_space=pltpu.SMEM)],
        out_shape=jax.ShapeDtypeStruct((rows * cols, x_rows * cols), BF16),
        compiler_params=pltpu.CompilerParams(vmem_limit_bytes=SMALL_BYTES),
        cost_estimate=pl.CostEstimate(
            flops=5 * 10**9, bytes_accessed=4 * rows * cols * x_rows * cols, transcendentals=0
        ),
        name="widen",
    )(place)


def forward_kernel(live, place_ref, wide_ref, field_ref, send_ref, keep_ref, *edge_refs):
    x_rows, y_rows, cols, channels = field_ref.shape
    sent = send_ref.shape[1]
    waves = send_ref.shape[0]
    for place in range(y_rows):
        row = jnp.where(place_ref[0] >> 1 & 1 == 0, (place + sent) % y_rows, place)
        part = jnp.dot(
            wide_ref[...],
            field_ref[:, row].reshape(x_rows * cols, channels),
            preferred_element_type=F32,
        ).reshape(waves, cols, channels)
        if place < sent:
            send_ref[:, place] = part.astype(BF16)
        else:
            keep_ref[:, place - sent] = part
    odd = place_ref[0] & 1
    for p, ref in zip(live, edge_refs):
        ref[...] = field_ref[:, (odd if p else 1 - odd) * (y_rows - 1)]


def forward_transform(features, wide, place, live):
    x_rows, y_rows, cols, channels = features.shape
    shape = (wide.shape[0] // cols, y_rows // 2, cols, channels)
    vmem = pl.BlockSpec(memory_space=pltpu.VMEM)
    smem = pl.BlockSpec(memory_space=pltpu.SMEM)
    return pl.pallas_call(
        functools.partial(forward_kernel, live),
        in_specs=[smem, vmem, vmem],
        out_specs=[vmem] * (2 + len(live)),
        out_shape=[
            jax.ShapeDtypeStruct(shape, BF16),
            jax.ShapeDtypeStruct(shape, F32),
            *[jax.ShapeDtypeStruct((x_rows, cols, channels), BF16) for _ in live],
        ],
        compiler_params=pltpu.CompilerParams(vmem_limit_bytes=SMALL_BYTES),
        name="forward",
    )(place, wide, features)


def hold_kernel(edge_ref, ahead_ref, out_ref):
    out_ref[...] = edge_ref[...]


def hold(edge, ahead):
    vmem = pl.BlockSpec(memory_space=pltpu.VMEM)
    return pl.pallas_call(
        hold_kernel,
        in_specs=[vmem, pl.BlockSpec(memory_space=pl.ANY)],
        out_specs=vmem,
        out_shape=jax.ShapeDtypeStruct(edge.shape, BF16),
        compiler_params=pltpu.CompilerParams(vmem_limit_bytes=SMALL_BYTES),
        name="hold",
    )(edge, ahead)


def first_mode(gx, halving, modes):
    return sum((gx >> level & 1) * (modes >> level) for level in range(1, halving))


def prepare_kernel(halving, total, place_ref, weight_ref, inv_ref, own_ref, sem):
    owned = own_ref.shape[0]
    first = first_mode(place_ref[0] >> 1, halving, weight_ref.shape[0])
    move = pltpu.make_async_copy(weight_ref.at[pl.ds(first, owned)], own_ref, sem)
    move.start()
    modes = weight_ref.shape[0]
    cols = inv_ref.shape[1] // (2 * modes)
    x_rows = inv_ref.shape[0] // cols
    table = wave_table(place_ref[0] >> 1, halving, modes, x_rows, total, True)
    xb = min(x_rows, 128)
    for part in range(x_rows // xb):
        inv_ref[part * xb * cols : (part + 1) * xb * cols] = spread(
            table[:, part * xb : (part + 1) * xb], cols
        )
    move.wait()


def prepare(x_rows, cols, weight, place, halving, total):
    modes = weight.shape[0]
    vmem = pl.BlockSpec(memory_space=pltpu.VMEM)
    return pl.pallas_call(
        functools.partial(prepare_kernel, halving, total),
        in_specs=[
            pl.BlockSpec(memory_space=pltpu.SMEM),
            pl.BlockSpec(memory_space=pltpu.HBM),
        ],
        out_specs=[vmem, vmem],
        out_shape=[
            jax.ShapeDtypeStruct((x_rows * cols, 2 * modes * cols), BF16),
            jax.ShapeDtypeStruct((modes >> halving - 1,) + weight.shape[1:], BF16),
        ],
        scratch_shapes=[pltpu.SemaphoreType.DMA],
        compiler_params=pltpu.CompilerParams(vmem_limit_bytes=SMALL_BYTES),
        name="prepare",
    )(place, weight)


def halve_kernel(half, keep_ref, got_ref, *refs):
    send_ref, next_ref = refs[-2:]
    next_ref[...] = keep_ref[:half] + got_ref[:half].astype(F32)
    send_ref[...] = (keep_ref[half:] + got_ref[half:].astype(F32)).astype(BF16)


def add_kernel(keep_ref, got_ref, *refs):
    send_ref, next_ref = refs[-2:]
    total = keep_ref[...] + got_ref[...].astype(F32)
    next_ref[...] = total
    send_ref[...] = total.astype(BF16)


def combine(keep, got, halve, ahead):
    half = keep.shape[0] // 2 if halve else keep.shape[0]
    shape = (half,) + keep.shape[1:]
    vmem = pl.BlockSpec(memory_space=pltpu.VMEM)
    return pl.pallas_call(
        functools.partial(halve_kernel, half) if halve else add_kernel,
        in_specs=[vmem, vmem] + [pl.BlockSpec(memory_space=pl.ANY)] * len(ahead),
        out_specs=[vmem, vmem],
        out_shape=[jax.ShapeDtypeStruct(shape, BF16), jax.ShapeDtypeStruct(shape, F32)],
        compiler_params=pltpu.CompilerParams(vmem_limit_bytes=SMALL_BYTES),
        name="halve" if halve else "add",
    )(keep, got, *ahead)


def join_kernel(mine_ref, got_ref, out_ref):
    half = mine_ref.shape[0]
    out_ref[:half] = mine_ref[...]
    out_ref[half:] = got_ref[...]


def join(mine, got):
    return pl.pallas_call(
        join_kernel,
        out_shape=jax.ShapeDtypeStruct((2 * mine.shape[0],) + mine.shape[1:], BF16),
        compiler_params=pltpu.CompilerParams(vmem_limit_bytes=SMALL_BYTES),
        name="join",
    )(mine, got)


def stack_kernel(*refs):
    out_ref = refs[-1]
    rows, _, channels = out_ref.shape
    at = 0
    for ref in refs[:-1]:
        count = ref.shape[0] * ref.shape[2]
        for row in range(rows):
            out_ref[row, at : at + count] = ref[:, row].reshape(count, channels)
        at += count


def stack_modes(pieces):
    waves = sum(p.shape[0] for p in pieces)
    _, rows, cols, channels = pieces[0].shape
    return pl.pallas_call(
        stack_kernel,
        out_shape=jax.ShapeDtypeStruct((rows, waves * cols, channels), BF16),
        compiler_params=pltpu.CompilerParams(vmem_limit_bytes=SMALL_BYTES),
        name="stack",
    )(*pieces)


def mix_kernel(keep_ref, got_ref, weight_ref, out_ref):
    modes = weight_ref.shape[0]
    _, rows, cols, channels = keep_ref.shape
    count = rows * cols
    dot = functools.partial(jnp.dot, preferred_element_type=F32)
    for mode in range(modes):
        both = slice(2 * mode, 2 * mode + 2)
        parts = keep_ref[both] + got_ref[both].astype(F32)
        parts = parts.reshape(2 * count, channels).astype(BF16)
        by_real = dot(parts, weight_ref[mode, 0])
        by_imag = dot(parts, weight_ref[mode, 1])
        mixed_real = by_real[:count] - by_imag[count:]
        mixed_imag = by_imag[:count] + by_real[count:]
        out_ref[2 * mode] = mixed_real.reshape(rows, cols, channels).astype(BF16)
        out_ref[2 * mode + 1] = mixed_imag.reshape(rows, cols, channels).astype(BF16)


def mix(keep, got, weight):
    return pl.pallas_call(
        mix_kernel,
        out_shape=jax.ShapeDtypeStruct(keep.shape, BF16),
        compiler_params=pltpu.CompilerParams(vmem_limit_bytes=SMALL_BYTES),
        name="mix",
    )(keep, got, weight)


BEFORE, HERE, AFTER, BLOCK, PLACE, GROUP, HALO, FLIP, DROP = range(9)


def row_kernel(
    halos, sub, items_ref, place_ref, field_ref, inv_ref, taps_ref,
    w_in_ref, bias_in_ref, w_out_ref, bias_out_ref, mine_ref, other_ref, *rest
):
    halo_refs = rest[:halos]
    out_ref, mixed_ref, joined_ref, hidden_ref = rest[-4:]
    xb = out_ref.shape[0]
    cols, channels = out_ref.shape[-2:]
    tokens = xb * cols
    field = lambda which: items_ref[place_ref[0] & 3, which, pl.program_id(0)]

    @pl.when(field(GROUP) == 0)
    def _():
        mixed_ref[...] = mine_ref[field(PLACE)]

    @pl.when(field(GROUP) == 1)
    def _():
        mixed_ref[...] = other_ref[field(PLACE)]

    start = field(BLOCK) * xb
    before, here, after = field(BEFORE), field(HERE), field(AFTER)
    taps = taps_ref[...]
    flip = field(FLIP) == 1
    tap_before = jnp.where(flip, taps[2:3], taps[0:1]).astype(BF16)
    tap_here = taps[1:2].astype(BF16)
    tap_after = jnp.where(flip, taps[0:1], taps[2:3])
    tap_after = jnp.where(field(DROP) == 1, 0.0, tap_after).astype(BF16)
    source = field(HALO)

    def load(row, s):
        return field_ref[pl.ds(start + s * sub // cols, sub // cols), row].reshape(sub, channels)

    def load_after(s):
        part = load(after, s)
        for at, ref in enumerate(halo_refs):
            halo = ref[pl.ds(start + s * sub // cols, sub // cols)].reshape(sub, channels)
            part = jnp.where(source == at + 1, halo, part)
        return part

    def join(s):
        rows = slice(s * sub, (s + 1) * sub)
        lines = pl.ds(pl.multiple_of(start * cols, xb * cols) + s * sub, sub)
        spectral = jnp.dot(inv_ref[lines], mixed_ref[...], preferred_element_type=F32)
        conv = (
            tap_before * load(before, s) + tap_here * load(here, s) + tap_after * load_after(s)
        )
        joined_ref[rows] = (spectral + conv.astype(F32)).astype(BF16)

    def expand(s):
        rows = slice(s * sub, (s + 1) * sub)
        x = jnp.dot(joined_ref[rows], w_in_ref[...], preferred_element_type=F32)
        x = (x + bias_in_ref[...]).astype(BF16)
        u = x * (BF16(GELU_A) + BF16(GELU_B) * (x * x))
        hidden_ref[rows] = x + x * jnp.tanh(u)

    def project(s):
        rows = slice(s * sub, (s + 1) * sub)
        y = jnp.dot(hidden_ref[rows], w_out_ref[...], preferred_element_type=F32)
        y = load(here, s).astype(F32) + (0.5 * y + bias_out_ref[...])
        out_ref[s * sub // cols : (s + 1) * sub // cols] = y.reshape(
            (sub // cols,) + out_ref.shape[1:]
        ).astype(BF16)

    parts = tokens // sub
    for s in range(parts + 2):
        if s < parts:
            join(s)
        if 0 <= s - 1 < parts:
            expand(s - 1)
        if s >= 2:
            project(s - 2)


def rows_of(out, field, inv, items, place, taps, dense, mixed, halos, xb, sub):
    x_rows, y_rows, cols, channels = field.shape
    w_in, bias_in, w_out, bias_out = dense
    hidden = w_in.shape[1]
    waves_cols = inv.shape[1]
    count = items.shape[2]
    tokens = xb * cols
    args = [
        items, place, field, inv, taps, w_in, bias_in, w_out, bias_out, *mixed, *halos,
    ]
    in_specs = [pl.BlockSpec(memory_space=pltpu.VMEM)] * (len(args) - 2)
    aliases = {}
    if out is not None:
        aliases = {len(args): 0}
        in_specs.append(pl.BlockSpec(memory_space=pl.ANY))
        args.append(out)
    return pl.pallas_call(
        functools.partial(row_kernel, len(halos), min(sub, tokens)),
        grid_spec=pltpu.PrefetchScalarGridSpec(
            num_scalar_prefetch=2,
            grid=(count,),
            in_specs=in_specs,
            out_specs=pl.BlockSpec(
                (xb, 1, cols, channels), lambda i, r, v: (r[v[0] & 3, BLOCK, i], r[v[0] & 3, HERE, i], 0, 0)
            ),
            scratch_shapes=[
                pltpu.VMEM((waves_cols, channels), BF16),
                pltpu.VMEM((tokens, channels), BF16),
                pltpu.VMEM((tokens, hidden), BF16),
            ],
        ),
        out_shape=jax.ShapeDtypeStruct(field.shape, BF16),
        input_output_aliases=aliases,
        compiler_params=pltpu.CompilerParams(vmem_limit_bytes=ROWS_BYTES),
        cost_estimate=pl.CostEstimate(
            flops=2 * count * tokens * channels * (2 * hidden + waves_cols),
            bytes_accessed=2 * count * tokens * channels,
            transcendentals=count * tokens * hidden,
        ),
        name="rows",
    )(*args)


def local(features, spectral_weight, conv_taps, w_in, bias_in, w_out, bias_out):
    x_rows, y_rows, cols, channels = features.shape
    modes = spectral_weight.shape[0]
    gx_size = lax.axis_size("gx")
    gy_size = lax.axis_size("gy")
    gx = lax.axis_index("gx")
    gy = lax.axis_index("gy")

    half_rows = y_rows // 2
    place = (gx * 2 + gy % 2).reshape(1)
    variants = [(odd, core) for core in range(2) for odd in range(2)]
    edges_of = lambda odd: [0 if odd else y_rows - 1, y_rows - 1 if odd else 0]
    live = [p for p in range(2) if gy_size > p + 1]

    levels = gx_size.bit_length() - 1
    halving = max(min(levels - 1, modes.bit_length()), 1)
    total = x_rows * gx_size
    swap = lambda a, level: lax.ppermute(
        a, "gx", [(i, i ^ (1 << level)) for i in range(gx_size)]
    )
    parts = half_rows
    xb = x_rows // parts
    halos = []
    send, keep, *edge = forward_transform(
        features, widen(place, halving, modes, cols, x_rows, total), place, live
    )
    inv, weight = prepare(x_rows, cols, spectral_weight, place, halving, total)
    for level in range(levels):
        got = swap(send, level)
        ahead = []
        if level == 0:
            for p, row in zip(live, edge):
                pairs = [(i, i + 1) for i in range(p, gy_size - 1, 2)]
                ahead.append(hold(row, send))
                halos.append(lax.ppermute(ahead[-1], "gy", pairs + [(b, a) for a, b in pairs]))
        if level + 1 < levels:
            ahead += [weight] if level == levels - 2 else []
            send, keep = combine(keep, got, level + 1 < halving, ahead)
    mixed = mix(keep, got, weight)
    for level in reversed(range(2, halving)):
        mixed = join(mixed, swap(mixed, level))
    mixed = [stack_modes([mixed, swap(mixed, 1)] if halving > 1 else [mixed])]
    mixed.append(swap(mixed[0], 0))

    def block_of(core, before, here, after, part, halo=0, flip=0, drop=0):
        group = 0 if here // half_rows == core else 1
        return before, here, after, part, here % half_rows, group, halo, flip, drop

    def calls_of(odd, core):
        calls = [[], []]
        for row in range(1, y_rows - 1):
            for part in range(parts):
                calls[0].append(block_of(core, row - 1, row, row + 1, part))
        for p, edge in reversed(list(enumerate(edges_of(odd)))):
            inner, flip = (1, 1) if edge == 0 else (y_rows - 2, 0)
            for part in range(parts):
                halo = live.index(p) + 1 if p in live else 0
                calls[1 if halo else 0].append(
                    block_of(core, inner, edge, edge, part, halo, flip, 0 if halo else 1)
                )
        return calls

    every = [calls_of(odd, core) for odd, core in variants]
    dense = (w_in, bias_in[None], w_out, bias_out[None])
    out = None
    for call in range(2 if live else 1):
        items = jnp.array([list(zip(*calls[call])) for calls in every], jnp.int32)
        out = rows_of(
            out, features, inv, items, place, conv_taps, dense, mixed, halos if call else [], xb, 512
        )
    return out


def solution(mesh):
    return jax.shard_map(
        local,
        mesh=mesh,
        in_specs=(P("gx", "gy", None, None), P(), P(), P(), P(), P(), P()),
        out_specs=P("gx", "gy", None, None),
        check_vma=False,
    )
```

```python
import functools
import math

import jax
import jax.numpy as jnp
from jax import lax
from jax.experimental import pallas as pl
from jax.experimental.pallas import tpu as pltpu
from jax.sharding import PartitionSpec as P

F32 = jnp.float32
BF16 = jnp.bfloat16
GELU_A = math.sqrt(2.0 / math.pi)
GELU_B = GELU_A * 0.044715
SMALL_BYTES = 16 * 2**20
ROWS_BYTES = 36 * 2**20


def wave_table(gx, halving, modes, x_rows, total, inverse):
    shape = (2 * modes, x_rows)
    row = lax.broadcasted_iota(jnp.int32, shape, 0)
    waves = row // 2 ^ first_mode(gx, halving, modes)
    product = waves * (gx * x_rows + lax.broadcasted_iota(jnp.int32, shape, 1)) % total
    angles = 2.0 * math.pi / total * product.astype(F32)
    parts = jnp.where(row % 2 == 0, jnp.cos(angles), -jnp.sin(angles))
    if inverse:
        parts = jnp.where(waves == 0, 1.0, 2.0) * parts
    return (parts * (1.0 / math.sqrt(total))).astype(BF16)


def spread(table, cols):
    waves, xb = table.shape
    columns = waves * cols
    place = (
        lax.broadcasted_iota(jnp.int32, (waves, columns), 1) // cols
        == lax.broadcasted_iota(jnp.int32, (waves, columns), 0)
    )
    tall = lax.dot_general(
        table, place.astype(F32).astype(BF16), (((0,), (0,)), ((), ())), preferred_element_type=F32
    )
    same = lax.broadcasted_iota(jnp.int32, (1, cols, columns), 2) % cols == lax.broadcasted_iota(
        jnp.int32, (1, cols, columns), 1
    )
    return jnp.where(same, tall[:, None, :], 0.0).reshape(xb * cols, columns).astype(BF16)


def spread_wide(table, cols):
    waves, xb = table.shape
    width = xb * cols
    place = (
        lax.broadcasted_iota(jnp.int32, (xb, width), 1) // cols
        == lax.broadcasted_iota(jnp.int32, (xb, width), 0)
    )
    wide = jnp.dot(table, place.astype(F32).astype(BF16), preferred_element_type=F32)
    same = lax.broadcasted_iota(jnp.int32, (1, cols, width), 2) % cols == lax.broadcasted_iota(
        jnp.int32, (1, cols, width), 1
    )
    return jnp.where(same, wide[:, None, :], 0.0).reshape(waves * cols, width).astype(BF16)


def widen_kernel(halving, modes, total, place_ref, wide_ref):
    cols = wide_ref.shape[0] // (2 * modes)
    x_rows = wide_ref.shape[1] // cols
    table = wave_table(place_ref[0] >> 1, halving, modes, x_rows, total, False)
    xb = min(x_rows, 128)
    width = xb * cols
    for part in range(x_rows // xb):
        wide_ref[:, part * width : (part + 1) * width] = spread_wide(
            table[:, part * xb : (part + 1) * xb], cols
        )


def widen(place, halving, modes, cols, x_rows, total):
    rows = 2 * modes
    return pl.pallas_call(
        functools.partial(widen_kernel, halving, modes, total),
        in_specs=[pl.BlockSpec(memory_space=pltpu.SMEM)],
        out_shape=jax.ShapeDtypeStruct((rows * cols, x_rows * cols), BF16),
        compiler_params=pltpu.CompilerParams(vmem_limit_bytes=SMALL_BYTES),
        cost_estimate=pl.CostEstimate(
            flops=5 * 10**9, bytes_accessed=4 * rows * cols * x_rows * cols, transcendentals=0
        ),
        name="widen",
    )(place)


def forward_kernel(live, place_ref, wide_ref, field_ref, send_ref, keep_ref, *edge_refs):
    x_rows, y_rows, cols, channels = field_ref.shape
    sent = send_ref.shape[1]
    waves = send_ref.shape[0]
    for place in range(y_rows):
        row = jnp.where(place_ref[0] >> 1 & 1 == 0, (place + sent) % y_rows, place)
        part = jnp.dot(
            wide_ref[...],
            field_ref[:, row].reshape(x_rows * cols, channels),
            preferred_element_type=F32,
        ).reshape(waves, cols, channels)
        if place < sent:
            send_ref[:, place] = part.astype(BF16)
        else:
            keep_ref[:, place - sent] = part
    odd = place_ref[0] & 1
    for p, ref in zip(live, edge_refs):
        ref[...] = field_ref[:, (odd if p else 1 - odd) * (y_rows - 1)]


def forward_transform(features, wide, place, live):
    x_rows, y_rows, cols, channels = features.shape
    shape = (wide.shape[0] // cols, y_rows // 2, cols, channels)
    vmem = pl.BlockSpec(memory_space=pltpu.VMEM)
    smem = pl.BlockSpec(memory_space=pltpu.SMEM)
    return pl.pallas_call(
        functools.partial(forward_kernel, live),
        in_specs=[smem, vmem, vmem],
        out_specs=[vmem] * (2 + len(live)),
        out_shape=[
            jax.ShapeDtypeStruct(shape, BF16),
            jax.ShapeDtypeStruct(shape, F32),
            *[jax.ShapeDtypeStruct((x_rows, cols, channels), BF16) for _ in live],
        ],
        compiler_params=pltpu.CompilerParams(vmem_limit_bytes=SMALL_BYTES),
        name="forward",
    )(place, wide, features)


def hold_kernel(edge_ref, ahead_ref, out_ref):
    out_ref[...] = edge_ref[...]


def hold(edge, ahead):
    vmem = pl.BlockSpec(memory_space=pltpu.VMEM)
    return pl.pallas_call(
        hold_kernel,
        in_specs=[vmem, pl.BlockSpec(memory_space=pl.ANY)],
        out_specs=vmem,
        out_shape=jax.ShapeDtypeStruct(edge.shape, BF16),
        compiler_params=pltpu.CompilerParams(vmem_limit_bytes=SMALL_BYTES),
        name="hold",
    )(edge, ahead)


def first_mode(gx, halving, modes):
    return sum((gx >> level & 1) * (modes >> level) for level in range(1, halving))


def prepare_kernel(halving, total, place_ref, weight_ref, inv_ref, own_ref, sem):
    owned = own_ref.shape[0]
    first = first_mode(place_ref[0] >> 1, halving, weight_ref.shape[0])
    move = pltpu.make_async_copy(weight_ref.at[pl.ds(first, owned)], own_ref, sem)
    move.start()
    modes = weight_ref.shape[0]
    cols = inv_ref.shape[1] // (2 * modes)
    x_rows = inv_ref.shape[0] // cols
    table = wave_table(place_ref[0] >> 1, halving, modes, x_rows, total, True)
    xb = min(x_rows, 128)
    for part in range(x_rows // xb):
        inv_ref[part * xb * cols : (part + 1) * xb * cols] = spread(
            table[:, part * xb : (part + 1) * xb], cols
        )
    move.wait()


def prepare(x_rows, cols, weight, place, halving, total):
    modes = weight.shape[0]
    vmem = pl.BlockSpec(memory_space=pltpu.VMEM)
    return pl.pallas_call(
        functools.partial(prepare_kernel, halving, total),
        in_specs=[
            pl.BlockSpec(memory_space=pltpu.SMEM),
            pl.BlockSpec(memory_space=pltpu.HBM),
        ],
        out_specs=[vmem, vmem],
        out_shape=[
            jax.ShapeDtypeStruct((x_rows * cols, 2 * modes * cols), BF16),
            jax.ShapeDtypeStruct((modes >> halving - 1,) + weight.shape[1:], BF16),
        ],
        scratch_shapes=[pltpu.SemaphoreType.DMA],
        compiler_params=pltpu.CompilerParams(vmem_limit_bytes=SMALL_BYTES),
        name="prepare",
    )(place, weight)


def halve_kernel(half, keep_ref, got_ref, *refs):
    send_ref, next_ref = refs[-2:]
    next_ref[...] = keep_ref[:half] + got_ref[:half].astype(F32)
    send_ref[...] = (keep_ref[half:] + got_ref[half:].astype(F32)).astype(BF16)


def add_kernel(keep_ref, got_ref, *refs):
    send_ref, next_ref = refs[-2:]
    total = keep_ref[...] + got_ref[...].astype(F32)
    next_ref[...] = total
    send_ref[...] = total.astype(BF16)


def combine(keep, got, halve, ahead):
    half = keep.shape[0] // 2 if halve else keep.shape[0]
    shape = (half,) + keep.shape[1:]
    vmem = pl.BlockSpec(memory_space=pltpu.VMEM)
    return pl.pallas_call(
        functools.partial(halve_kernel, half) if halve else add_kernel,
        in_specs=[vmem, vmem] + [pl.BlockSpec(memory_space=pl.ANY)] * len(ahead),
        out_specs=[vmem, vmem],
        out_shape=[jax.ShapeDtypeStruct(shape, BF16), jax.ShapeDtypeStruct(shape, F32)],
        compiler_params=pltpu.CompilerParams(vmem_limit_bytes=SMALL_BYTES),
        name="halve" if halve else "add",
    )(keep, got, *ahead)


def join_kernel(mine_ref, got_ref, out_ref):
    half = mine_ref.shape[0]
    out_ref[:half] = mine_ref[...]
    out_ref[half:] = got_ref[...]


def join(mine, got):
    return pl.pallas_call(
        join_kernel,
        out_shape=jax.ShapeDtypeStruct((2 * mine.shape[0],) + mine.shape[1:], BF16),
        compiler_params=pltpu.CompilerParams(vmem_limit_bytes=SMALL_BYTES),
        name="join",
    )(mine, got)


def stack_kernel(*refs):
    out_ref = refs[-1]
    rows, _, channels = out_ref.shape
    at = 0
    for ref in refs[:-1]:
        count = ref.shape[0] * ref.shape[2]
        for row in range(rows):
            out_ref[row, at : at + count] = ref[:, row].reshape(count, channels)
        at += count


def stack_modes(pieces):
    waves = sum(p.shape[0] for p in pieces)
    _, rows, cols, channels = pieces[0].shape
    return pl.pallas_call(
        stack_kernel,
        out_shape=jax.ShapeDtypeStruct((rows, waves * cols, channels), BF16),
        compiler_params=pltpu.CompilerParams(vmem_limit_bytes=SMALL_BYTES),
        name="stack",
    )(*pieces)


def mix_kernel(keep_ref, got_ref, weight_ref, out_ref):
    modes = weight_ref.shape[0]
    _, rows, cols, channels = keep_ref.shape
    count = rows * cols
    dot = functools.partial(jnp.dot, preferred_element_type=F32)
    for mode in range(modes):
        both = slice(2 * mode, 2 * mode + 2)
        parts = keep_ref[both] + got_ref[both].astype(F32)
        parts = parts.reshape(2 * count, channels).astype(BF16)
        by_real = dot(parts, weight_ref[mode, 0])
        by_imag = dot(parts, weight_ref[mode, 1])
        mixed_real = by_real[:count] - by_imag[count:]
        mixed_imag = by_imag[:count] + by_real[count:]
        out_ref[2 * mode] = mixed_real.reshape(rows, cols, channels).astype(BF16)
        out_ref[2 * mode + 1] = mixed_imag.reshape(rows, cols, channels).astype(BF16)


def mix(keep, got, weight):
    return pl.pallas_call(
        mix_kernel,
        out_shape=jax.ShapeDtypeStruct(keep.shape, BF16),
        compiler_params=pltpu.CompilerParams(vmem_limit_bytes=SMALL_BYTES),
        name="mix",
    )(keep, got, weight)


BEFORE, HERE, AFTER, BLOCK, PLACE, GROUP, HALO, FLIP, DROP = range(9)


def row_kernel(
    halos, sub, items_ref, place_ref, field_ref, inv_ref, taps_ref,
    w_in_ref, bias_in_ref, w_out_ref, bias_out_ref, mine_ref, other_ref, *rest
):
    halo_refs = rest[:halos]
    out_ref, mixed_ref, joined_ref, hidden_ref = rest[-4:]
    xb = out_ref.shape[0]
    cols, channels = out_ref.shape[-2:]
    tokens = xb * cols
    field = lambda which: items_ref[place_ref[0] & 3, which, pl.program_id(0)]

    @pl.when(field(GROUP) == 0)
    def _():
        mixed_ref[...] = mine_ref[field(PLACE)]

    @pl.when(field(GROUP) == 1)
    def _():
        mixed_ref[...] = other_ref[field(PLACE)]

    start = field(BLOCK) * xb
    before, here, after = field(BEFORE), field(HERE), field(AFTER)
    taps = taps_ref[...]
    flip = field(FLIP) == 1
    tap_before = jnp.where(flip, taps[2:3], taps[0:1]).astype(BF16)
    tap_here = taps[1:2].astype(BF16)
    tap_after = jnp.where(flip, taps[0:1], taps[2:3])
    tap_after = jnp.where(field(DROP) == 1, 0.0, tap_after).astype(BF16)
    source = field(HALO)

    def load(row, s):
        return field_ref[pl.ds(start + s * sub // cols, sub // cols), row].reshape(sub, channels)

    def load_after(s):
        lines = pl.ds(start + s * sub // cols, sub // cols)
        parts = [ref[lines].reshape(sub, channels) for ref in halo_refs] or [load(after, s)]
        part = parts[0]
        for at, other in enumerate(parts[1:]):
            part = jnp.where(source == at + 2, other, part)
        return part

    def join(s):
        rows = slice(s * sub, (s + 1) * sub)
        lines = pl.ds(pl.multiple_of(start * cols, xb * cols) + s * sub, sub)
        spectral = jnp.dot(inv_ref[lines], mixed_ref[...], preferred_element_type=F32)
        conv = (
            tap_before * load(before, s) + tap_here * load(here, s) + tap_after * load_after(s)
        )
        joined_ref[rows] = (spectral + conv.astype(F32)).astype(BF16)

    def expand(s):
        rows = slice(s * sub, (s + 1) * sub)
        x = jnp.dot(joined_ref[rows], w_in_ref[...], preferred_element_type=F32)
        x = (x + bias_in_ref[...]).astype(BF16)
        u = x * (BF16(GELU_A) + BF16(GELU_B) * (x * x))
        hidden_ref[rows] = x + x * jnp.tanh(u)

    def project(s):
        rows = slice(s * sub, (s + 1) * sub)
        y = jnp.dot(hidden_ref[rows], w_out_ref[...], preferred_element_type=F32)
        y = load(here, s).astype(F32) + (0.5 * y + bias_out_ref[...])
        out_ref[s * sub // cols : (s + 1) * sub // cols] = y.reshape(
            (sub // cols,) + out_ref.shape[1:]
        ).astype(BF16)

    parts = tokens // sub
    for s in range(parts + 2):
        if s < parts:
            join(s)
        if 0 <= s - 1 < parts:
            expand(s - 1)
        if s >= 2:
            project(s - 2)


def rows_of(out, field, inv, items, place, taps, dense, mixed, halos, xb, sub):
    x_rows, y_rows, cols, channels = field.shape
    w_in, bias_in, w_out, bias_out = dense
    hidden = w_in.shape[1]
    waves_cols = inv.shape[1]
    count = items.shape[2]
    tokens = xb * cols
    args = [
        items, place, field, inv, taps, w_in, bias_in, w_out, bias_out, *mixed, *halos,
    ]
    in_specs = [pl.BlockSpec(memory_space=pltpu.VMEM)] * (len(args) - 2)
    aliases = {}
    if out is not None:
        aliases = {len(args): 0}
        in_specs.append(pl.BlockSpec(memory_space=pl.ANY))
        args.append(out)
    return pl.pallas_call(
        functools.partial(row_kernel, len(halos), min(sub, tokens)),
        grid_spec=pltpu.PrefetchScalarGridSpec(
            num_scalar_prefetch=2,
            grid=(count,),
            in_specs=in_specs,
            out_specs=pl.BlockSpec(
                (xb, 1, cols, channels), lambda i, r, v: (r[v[0] & 3, BLOCK, i], r[v[0] & 3, HERE, i], 0, 0)
            ),
            scratch_shapes=[
                pltpu.VMEM((waves_cols, channels), BF16),
                pltpu.VMEM((tokens, channels), BF16),
                pltpu.VMEM((tokens, hidden), BF16),
            ],
        ),
        out_shape=jax.ShapeDtypeStruct(field.shape, BF16),
        input_output_aliases=aliases,
        compiler_params=pltpu.CompilerParams(vmem_limit_bytes=ROWS_BYTES),
        cost_estimate=pl.CostEstimate(
            flops=2 * count * tokens * channels * (2 * hidden + waves_cols),
            bytes_accessed=2 * count * tokens * channels,
            transcendentals=count * tokens * hidden,
        ),
        name="rows",
    )(*args)


def local(features, spectral_weight, conv_taps, w_in, bias_in, w_out, bias_out):
    x_rows, y_rows, cols, channels = features.shape
    modes = spectral_weight.shape[0]
    gx_size = lax.axis_size("gx")
    gy_size = lax.axis_size("gy")
    gx = lax.axis_index("gx")
    gy = lax.axis_index("gy")

    half_rows = y_rows // 2
    place = (gx * 2 + gy % 2).reshape(1)
    variants = [(odd, core) for core in range(2) for odd in range(2)]
    edges_of = lambda odd: [0 if odd else y_rows - 1, y_rows - 1 if odd else 0]
    live = [p for p in range(2) if gy_size > p + 1]

    levels = gx_size.bit_length() - 1
    halving = max(min(levels - 1, modes.bit_length()), 1)
    total = x_rows * gx_size
    swap = lambda a, level: lax.ppermute(
        a, "gx", [(i, i ^ (1 << level)) for i in range(gx_size)]
    )
    parts = half_rows
    xb = x_rows // parts
    halos = []
    send, keep, *edge = forward_transform(
        features, widen(place, halving, modes, cols, x_rows, total), place, live
    )
    inv, weight = prepare(x_rows, cols, spectral_weight, place, halving, total)
    for level in range(levels):
        got = swap(send, level)
        ahead = []
        if level == 0:
            for p, row in zip(live, edge):
                pairs = [(i, i + 1) for i in range(p, gy_size - 1, 2)]
                ahead.append(hold(row, send))
                halos.append(lax.ppermute(ahead[-1], "gy", pairs + [(b, a) for a, b in pairs]))
        if level + 1 < levels:
            ahead += [weight] if level == levels - 2 else []
            send, keep = combine(keep, got, level + 1 < halving, ahead)
    mixed = mix(keep, got, weight)
    for level in reversed(range(2, halving)):
        mixed = join(mixed, swap(mixed, level))
    mixed = [stack_modes([mixed, swap(mixed, 1)] if halving > 1 else [mixed])]
    mixed.append(swap(mixed[0], 0))

    def block_of(core, before, here, after, part, halo=0, flip=0, drop=0):
        group = 0 if here // half_rows == core else 1
        return before, here, after, part, here % half_rows, group, halo, flip, drop

    def calls_of(odd, core):
        calls = [[], []]
        for row in range(1, y_rows - 1):
            for part in range(parts):
                calls[0].append(block_of(core, row - 1, row, row + 1, part))
        for p, edge in reversed(list(enumerate(edges_of(odd)))):
            inner, flip = (1, 1) if edge == 0 else (y_rows - 2, 0)
            for part in range(parts):
                halo = live.index(p) + 1 if p in live else 0
                calls[1 if halo else 0].append(
                    block_of(core, inner, edge, edge, part, halo, flip, 0 if halo else 1)
                )
        return calls

    every = [calls_of(odd, core) for odd, core in variants]
    dense = (w_in, bias_in[None], w_out, bias_out[None])
    out = None
    for call in range(2 if live else 1):
        items = jnp.array([list(zip(*calls[call])) for calls in every], jnp.int32)
        out = rows_of(
            out, features, inv, items, place, conv_taps, dense, mixed, halos if call else [], xb, 512
        )
    return out


def solution(mesh):
    return jax.shard_map(
        local,
        mesh=mesh,
        in_specs=(P("gx", "gy", None, None), P(), P(), P(), P(), P(), P()),
        out_specs=P("gx", "gy", None, None),
        check_vma=False,
    )
```
